128 devices in a mesh: tm: 16 (over z, y), space: 8 (over x, core).
Axes of the slice: x: 4, y: 4, z: 4, core: 2. Of those that a mesh axis runs over, the one named last changes fastest.
Arguments:
- state: float32 [2048, 8192], P('tm', 'space'), may hold values from -4 to 4
- space_factor: bfloat16 [8192, 8192], P('space'), as said below
- time_factor: float32 [2048, 2048], replicated, as said below
- footprints: bfloat16 [1024, 8, 128, 256], P('tm', 'space'), may hold values from -0.125 to 0.125
- tile_obs: int32 [1024, 8], P('tm', 'space'), may hold values from 0 to 1023, as said below
- tile_block: int32 [1024, 8], P('tm', 'space'), may hold values from 0 to 31, as said below
- tile_time: int32 [1024, 8], P('tm', 'space'), may hold values from 0 to 2047
- tile_count: int32 [16, 8], P('tm', 'space'), may hold values from 8 to 64, as said below
- obs_dep: float32 [1024, 128], P('tm'), may hold values from -6 to 6
- obs_weight: float32 [1024, 128], P('tm'), may hold values from 0.25 to 4
Outputs:
- gradient: float32 [2048, 8192], P('tm', 'space')
The draws below stay inside these ranges and needn't reach their ends.
Inputs may be any that keep to these rules, and one draw needn't show every extreme that they name: `tile_obs`: the observation tile of a slot on tm index i lies among that index's own tiles, i * 64 to (i + 1) * 64 - 1. `tile_block`: the cell block of a slot on space index j lies in that index's cells, j * 4 to (j + 1) * 4 - 1. `tile_count`: some device has all 64 slots live. `space_factor`: the identity plus off-diagonal entries of half the identity's row weight. `time_factor`: the identity plus off-diagonal entries of half the identity's row weight.
All inputs are finite; a program needn't handle non-finite values.
Results may differ from the reference program's by a relative error of at most 0.0065.
Values may be sent and summed in bfloat16 or wider, within the bound.
A program may use at most 128 MiB of HBM per device.

```python
import math
import jax
import jax.numpy as jnp
from jax import lax

CELLS = 8192
TILE_OBS = 128
TILE_CELLS = 256
TILE_CAP = 64
OTILE_DEV = 64
NT = 2048
OTILES = 1024
TILES_TM = 1024
BLOCKS = 32
BLK_DEV = 4
N_TM = 16
N_SPACE = 8


def unit_factor(key, order):
    off_part = jax.random.normal(key, (order, order), jnp.float32) * (0.5 / math.sqrt(order))
    return off_part + jnp.eye(order, dtype=jnp.float32)


def draw_space_factor(key, part):
    key = jax.random.fold_in(key, 11)
    return unit_factor(key, CELLS).astype(jnp.bfloat16)


def draw_time_factor(key, part):
    key = jax.random.fold_in(key, 13)
    return unit_factor(key, NT)


def draw_tile_obs(key, part):
    key = jax.random.fold_in(key, 21)
    offsets = jax.random.randint(key, (N_TM, TILE_CAP, N_SPACE), 0, OTILE_DEV, jnp.int32)
    offsets = offsets.at[:, 0, :].set(OTILE_DEV - 1).at[:, 1, :].set(0)
    base_tile = jnp.arange(N_TM, dtype=jnp.int32)[:, None, None] * OTILE_DEV
    return (offsets + base_tile).reshape(TILES_TM, N_SPACE)


def draw_tile_block(key, part):
    key = jax.random.fold_in(key, 23)
    offsets = jax.random.randint(key, (N_TM, TILE_CAP, N_SPACE), 0, BLK_DEV, jnp.int32)
    offsets = offsets.at[:, 0, :].set(BLK_DEV - 1).at[:, 1, :].set(0)
    base_block = jnp.arange(N_SPACE, dtype=jnp.int32)[None, None, :] * BLK_DEV
    return (offsets + base_block).reshape(TILES_TM, N_SPACE)


def draw_tile_time(key, part):
    key = jax.random.fold_in(key, 29)
    times = jax.random.randint(key, (TILES_TM, N_SPACE), 0, NT, jnp.int32)
    return times.at[0, 0].set(NT - 1).at[1, 0].set(0)


def draw_tile_count(key, part):
    key = jax.random.fold_in(key, 31)
    first_key, second_key = jax.random.split(key)
    counts = jax.random.randint(first_key, (N_TM * N_SPACE,), TILE_CAP // 8, TILE_CAP + 1, jnp.int32)
    order = jax.random.permutation(second_key, N_TM * N_SPACE)
    counts = counts.at[order[0]].set(TILE_CAP).at[order[1]].set(TILE_CAP // 8)
    return counts.reshape(N_TM, N_SPACE)


def block_scale(stream_key, extent, cuts, least, top_value):
    factor_of = 1.0
    for dim, blocks in cuts:
        draws = jax.random.uniform(jax.random.fold_in(jax.random.fold_in(stream_key, 6), dim), (blocks,), jnp.float32, least / len(cuts), top_value / len(cuts))
        factor_of = factor_of * jnp.repeat(jnp.exp(draws), extent[dim] // blocks).reshape((-1,) + (1,) * (len(extent) - 1 - dim))
    return factor_of


def gaussian(stream_key, dims, scale, most, cuts=(), kind=jnp.bfloat16):
    entries = scale * jax.random.normal(stream_key, dims, jnp.float32)
    if cuts:
        entries = entries * block_scale(stream_key, dims, cuts, -0.22, 0.18)
    return jnp.clip(entries, -most, most).astype(kind)


def setup_inputs(seed: int = 0) -> dict:
    arg_keys = jax.random.split(jax.random.key(seed), 11)
    state = gaussian(arg_keys[0], (NT, CELLS), 0.5, 4.0, ((0, 16), (1, 8)), jnp.float32)
    space_factor = draw_space_factor(jax.random.fold_in(arg_keys[10], 71), 0)
    time_factor = draw_time_factor(jax.random.fold_in(arg_keys[10], 71), 0)
    footprints = gaussian(arg_keys[3], (TILES_TM, N_SPACE, TILE_OBS, TILE_CELLS), (TILE_CELLS * TILE_CAP * N_SPACE // OTILE_DEV) ** -0.5, 0.125, ((0, 16), (1, 8)))
    tile_obs = draw_tile_obs(jax.random.fold_in(arg_keys[10], 71), 0)
    tile_block = draw_tile_block(jax.random.fold_in(arg_keys[10], 71), 0)
    tile_time = draw_tile_time(jax.random.fold_in(arg_keys[10], 71), 0)
    tile_count = draw_tile_count(jax.random.fold_in(arg_keys[10], 71), 0)
    obs_dep = gaussian(arg_keys[8], (OTILES, TILE_OBS), 1.0, 6.0, ((0, 16),), jnp.float32)
    obs_weight = jnp.clip(jnp.exp(math.log(4.0) - 2.7725887 * jax.random.uniform(arg_keys[9], (OTILES, TILE_OBS), jnp.float32) ** block_scale(arg_keys[9], (OTILES, TILE_OBS), ((0, 16),), -0.2, 0.2)), 0.25, 4.0)
    return {"state": state, "space_factor": space_factor, "time_factor": time_factor, "footprints": footprints, "tile_obs": tile_obs, "tile_block": tile_block, "tile_time": tile_time, "tile_count": tile_count, "obs_dep": obs_dep, "obs_weight": obs_weight}


def reference(state, space_factor, time_factor, footprints, tile_obs, tile_block, tile_time, tile_count, obs_dep, obs_weight):
    highest = lax.Precision.HIGHEST
    state_low = state.astype(jnp.bfloat16)
    spread = jnp.dot(state_low, space_factor.T, preferred_element_type=jnp.float32)
    flux = jnp.dot(time_factor, spread, precision=highest)
    flux_low = flux.astype(jnp.bfloat16).reshape(NT, BLOCKS, TILE_CELLS)
    tile_maps = footprints.reshape(N_TM, TILE_CAP, N_SPACE, TILE_OBS, TILE_CELLS)
    obs_index = tile_obs.reshape(N_TM, TILE_CAP, N_SPACE)
    block_index = tile_block.reshape(N_TM, TILE_CAP, N_SPACE)
    time_index = tile_time.reshape(N_TM, TILE_CAP, N_SPACE)
    slots = jnp.arange(TILE_CAP, dtype=jnp.int32)
    live_mask = (slots[None, :, None] < tile_count[:, None, :]).astype(jnp.float32)

    def forward_group(inputs):
        maps_here, block_here, time_here, mask_here = inputs
        flux_cols = flux_low[time_here, block_here].astype(jnp.float32)
        sims = jnp.einsum("ksob,ksb->kso", maps_here.astype(jnp.float32), flux_cols)
        return sims * mask_here[..., None]

    tile_sims = lax.map(forward_group, (tile_maps, block_index, time_index, live_mask))
    evolved = jnp.zeros((OTILES, TILE_OBS), jnp.float32).at[obs_index.reshape(-1)].add(tile_sims.reshape(-1, TILE_OBS))
    depart_low = (obs_weight * (evolved - obs_dep)).astype(jnp.bfloat16)

    def adjoint_group(inputs):
        maps_here, obs_here, mask_here = inputs
        tile_depart = depart_low[obs_here].astype(jnp.float32)
        backs = jnp.einsum("ksob,kso->ksb", maps_here.astype(jnp.float32), tile_depart)
        return backs * mask_here[..., None]

    tile_back = lax.map(adjoint_group, (tile_maps, obs_index, live_mask))
    q_field = jnp.zeros((NT, BLOCKS, TILE_CELLS), jnp.float32)
    q_field = q_field.at[time_index.reshape(-1), block_index.reshape(-1)].add(tile_back.reshape(-1, TILE_CELLS))
    q_field = q_field.reshape(NT, CELLS)
    adjoint = jnp.dot(time_factor.T, q_field, precision=highest)
    adjoint_low = adjoint.astype(jnp.bfloat16)
    return state + jnp.dot(adjoint_low, space_factor, preferred_element_type=jnp.float32)
```

```python
import functools

import jax
import jax.numpy as jnp
from jax import lax
from jax.experimental import pallas as pl
from jax.experimental.pallas import tpu as pltpu
from jax.sharding import PartitionSpec as P

MESH = pl.DeviceIdType.MESH
F32 = jnp.float32
BF16 = jnp.bfloat16
NX = 4
NTM = 16
NSP = 8
SLOTS = 64
ROWS = 128
HALF = ROWS // 2
COLS = 1024
BLK = 256
NBLK = COLS // BLK
OBS = 128
TIMES = 2048
OWN, RIGHT, OPP, LEFT = 0, 1, 2, 3


def nt_dot(a, b):
    return lax.dot_general(a, b, (((1,), (1,)), ((), ())), preferred_element_type=F32)


def nn_dot(a, b):
    return jnp.dot(a, b, preferred_element_type=F32)


def kernel(
    state_hbm,
    space_hbm,
    time_hbm,
    foot_hbm,
    obs_hbm,
    block_hbm,
    when_hbm,
    count_hbm,
    dep_hbm,
    weight_hbm,
    out_hbm,
    state_v,
    space_v,
    time_v,
    foot_v,
    obs_v,
    block_v,
    when_v,
    count_v,
    dep_v,
    weight_v,
    out_v,
    xall,
    spread_v,
    time_t,
    meta_out,
    meta_in,
    gt4,
    g4,
    part_out,
    part_in,
    sims_v,
    evo_out,
    evo_in,
    back_out,
    back_in,
    adj_v,
    sib_out,
    sib_in,
    term_v,
    hop_out,
    hop_in,
    lsem,
    ssem,
    rsem,
):
    tm = lax.axis_index("tm")
    sp = lax.axis_index("space")
    z, y = lax.div(tm, NX), lax.rem(tm, NX)
    x, core = lax.div(sp, 2), lax.rem(sp, 2)
    other = 1 - core

    def at_x(rel, c):
        return lax.rem(x + rel, NX) * 2 + c

    def plus(e):
        dz, dy = divmod(e, NX)
        return lax.rem(z + dz, NX) * NX + lax.rem(y + dy, NX)

    def minus(e):
        dz, dy = divmod(e, NX)
        return lax.rem(z + NX - dz, NX) * NX + lax.rem(y + NX - dy, NX)

    loads = []

    def load(src, dst):
        copy = pltpu.make_async_copy(src, dst, lsem.at[len(loads)])
        copy.start()
        loads.append(copy)
        return copy

    sends = []

    def send(src, dst, **where):
        n = len(sends)
        copy = pltpu.make_async_remote_copy(
            src_ref=src,
            dst_ref=dst,
            send_sem=ssem.at[n],
            recv_sem=rsem.at[n],
            device_id=where,
            device_id_type=MESH,
        )
        copy.start()
        sends.append(copy)
        return copy

    ld_state = load(state_hbm, state_v)
    ld_when = load(when_hbm, when_v)
    ld_block = load(block_hbm, block_v)
    ld_count = load(count_hbm, count_v)
    ld_obs = load(obs_hbm, obs_v)

    def load_space(rel, c):
        cols = pl.ds(pl.multiple_of(at_x(rel, c) * COLS, COLS), COLS)
        return load(space_hbm.at[:, cols], space_v.at[rel, 0 if c is core else 1])

    ld_space = {}
    ld_space[OWN, 0] = load_space(OWN, core)
    ld_time = load(time_hbm.at[:, pl.ds(pl.multiple_of(tm * ROWS, ROWS), ROWS)], time_v)
    for rel in (OWN, RIGHT, LEFT, OPP):
        for c in (0, 1):
            if (rel, c) != (OWN, 0):
                ld_space[rel, c] = load_space(rel, other if c else core)
    ld_foot = load(foot_hbm, foot_v)
    ld_dep = load(dep_hbm, dep_v)
    ld_weight = load(weight_hbm, weight_v)

    barrier = pltpu.get_barrier_semaphore()
    for e in range(1, NTM):
        pl.semaphore_signal(barrier, inc=1, device_id={"tm": plus(e)}, device_id_type=MESH)
    for d in range(1, NSP):
        pl.semaphore_signal(
            barrier, inc=1, device_id={"space": lax.rem(sp + d, NSP)}, device_id_type=MESH
        )
    ld_state.wait()
    xall[OWN, 0] = state_v[...].astype(BF16)
    ld_when.wait()
    ld_block.wait()
    ld_count.wait()
    lane = lax.broadcasted_iota(jnp.int32, (1, SLOTS), 1)
    code = when_v[...] * 8 + (block_v[...] - sp * NBLK)
    code = jnp.where(lane < count_v[...], code, -8)
    zero = jnp.zeros((1, SLOTS), jnp.int32)
    meta_out[0] = jnp.broadcast_to(jnp.concatenate([code, zero], axis=1), (8, 2 * SLOTS))
    meta_out[1] = jnp.broadcast_to(jnp.concatenate([zero, code], axis=1), (8, 2 * SLOTS))
    meta_in[0] = meta_out[0]
    pl.semaphore_wait(barrier, NTM - 1 + NSP - 1)

    right, left = at_x(RIGHT, core), at_x(LEFT, core)
    sibling = at_x(OWN, other)
    top, low = pl.ds(0, HALF), pl.ds(HALF, HALF)

    from_left0 = send(xall.at[OWN, 0, top], xall.at[LEFT, 0, top], space=right)
    from_right1 = send(xall.at[OWN, 0, low], xall.at[RIGHT, 0, low], space=left)
    from_left1 = send(xall.at[OWN, 0, low], xall.at[LEFT, 0, low], space=right)
    from_right0 = send(xall.at[OWN, 0, top], xall.at[RIGHT, 0, top], space=left)
    from_sib = {OWN: [send(xall.at[OWN, 0], xall.at[OWN, 1], space=sibling)]}
    from_meta = [None] + [
        send(meta_out.at[e % 2], meta_in.at[e], tm=plus(e)) for e in range(1, NTM)
    ]

    def add_spread(rel, c, first=False):
        ld_space[rel, c].wait()

        @pl.loop(0, COLS // BLK)
        def _(n):
            cols = pl.ds(pl.multiple_of(n * BLK, BLK), BLK)
            term = nt_dot(xall[rel, c], space_v[rel, c, cols, :])
            if first:
                spread_v[:, cols] = term
            else:
                spread_v[:, cols] += term

    add_spread(OWN, 0, first=True)
    from_left0.wait_recv()
    from_opp0 = send(xall.at[LEFT, 0, top], xall.at[OPP, 0, top], space=right)
    from_right1.wait_recv()
    from_opp1 = send(xall.at[RIGHT, 0, low], xall.at[OPP, 0, low], space=left)
    from_sib[LEFT] = [send(xall.at[LEFT, 0, top], xall.at[LEFT, 1, top], space=sibling)]
    from_sib[RIGHT] = [send(xall.at[RIGHT, 0, low], xall.at[RIGHT, 1, low], space=sibling)]

    ld_time.wait()
    time_t[...] = time_v[...].T.astype(BF16)
    for e in range(1, NTM):
        from_meta[e].wait_recv()

    @pl.loop(0, NTM // 2)
    def _(m):
        row = meta_in[2 * m, 0:1, :] + meta_in[2 * m + 1, 0:1, :]
        when = lax.shift_right_arithmetic(row, 3)
        which = jnp.bitwise_and(row, 7)
        hot = lax.broadcasted_iota(jnp.int32, (TIMES, 2 * SLOTS), 0) == when
        picked = nn_dot(time_t[...], jnp.where(hot, 1.0, 0.0).astype(BF16))
        slots = pl.ds(pl.multiple_of(m * 2 * SLOTS, 2 * SLOTS), 2 * SLOTS)
        picked_t = picked.T
        which_t = jnp.broadcast_to(which.astype(F32), (2 * SLOTS, 2 * SLOTS)).T
        for b in range(NBLK):
            gt4[b * ROWS : (b + 1) * ROWS, slots] = jnp.where(which == b, picked, 0.0).astype(BF16)
            g4[slots, b * ROWS : (b + 1) * ROWS] = jnp.where(
                which_t == float(b), picked_t, 0.0
            ).astype(BF16)

    from_sib[OWN][0].wait_recv()
    add_spread(OWN, 1)
    from_left1.wait_recv()
    from_sib[LEFT].append(send(xall.at[LEFT, 0, low], xall.at[LEFT, 1, low], space=sibling))
    from_right0.wait_recv()
    from_sib[RIGHT].append(send(xall.at[RIGHT, 0, top], xall.at[RIGHT, 1, top], space=sibling))
    add_spread(LEFT, 0)
    add_spread(RIGHT, 0)
    for rel in (LEFT, RIGHT):
        for copy in from_sib[rel]:
            copy.wait_recv()
        add_spread(rel, 1)
    from_opp0.wait_recv()
    from_sib[OPP] = [send(xall.at[OPP, 0, top], xall.at[OPP, 1, top], space=sibling)]
    from_opp1.wait_recv()
    from_sib[OPP].append(send(xall.at[OPP, 0, low], xall.at[OPP, 1, low], space=sibling))
    add_spread(OPP, 0)
    for copy in from_sib[OPP]:
        copy.wait_recv()
    add_spread(OPP, 1)

    spread4 = jnp.concatenate(
        [spread_v[:, b * BLK : (b + 1) * BLK].astype(BF16) for b in range(NBLK)], axis=0
    )
    from_part = [None] * NTM
    for m in range(NTM // 2):
        part = nn_dot(g4[m * 2 * SLOTS : (m + 1) * 2 * SLOTS, :], spread4)
        part_out[2 * m : 2 * m + 2] = part.astype(BF16).reshape(2, SLOTS, BLK)
        for e in (2 * m, 2 * m + 1):
            if e:
                from_part[e] = send(part_out.at[e], part_in.at[e], tm=minus(e))
    flux = part_out[0].astype(F32)
    for e in range(1, NTM):
        from_part[e].wait_recv()
        flux += part_in[e].astype(F32)
    flux = flux.astype(BF16)

    ld_foot.wait()
    ld_obs.wait()
    group = 16
    row16 = lax.broadcasted_iota(jnp.int32, (group, BLK), 0)
    for g in range(SLOTS // group):
        mine = flux[g * group : (g + 1) * group, :]
        acc = jnp.zeros((group, OBS), F32)
        for k in range(group):
            acc += nt_dot(jnp.where(row16 == k, mine, jnp.zeros_like(mine)), foot_v[g * group + k])
        sims_v[g * group : (g + 1) * group, :] = acc
    sims = sims_v[...]
    pick = jnp.where(
        lax.broadcasted_iota(jnp.int32, (SLOTS, SLOTS), 0) == obs_v[...] - tm * SLOTS, 1.0, 0.0
    )
    pick_low = pick.astype(BF16)
    sims_hi = sims.astype(BF16)
    sims_lo = (sims - sims_hi.astype(F32)).astype(BF16)
    evolved = nn_dot(pick_low, sims_hi) + nn_dot(pick_low, sims_lo)
    evo_out[...] = evolved.astype(BF16)
    from_evo = [None] + [
        send(evo_out, evo_in.at[d], space=lax.rem(sp + d, NSP)) for d in range(1, NSP)
    ]
    pick_t = pick.T.astype(BF16)
    ld_dep.wait()
    ld_weight.wait()
    for d in range(1, NSP):
        from_evo[d].wait_recv()
        evolved += evo_in[d].astype(F32)
    depart = (weight_v[...] * (evolved - dep_v[...])).astype(BF16)
    mine_dep = nn_dot(pick_t, depart).astype(BF16)

    row16 = lax.broadcasted_iota(jnp.int32, (group, OBS), 0)
    for g in range(SLOTS // group):
        mine = mine_dep[g * group : (g + 1) * group, :]
        acc = jnp.zeros((group, BLK), F32)
        for k in range(group):
            acc += nn_dot(jnp.where(row16 == k, mine, jnp.zeros_like(mine)), foot_v[g * group + k])
        back_out[g * group : (g + 1) * group, :] = acc.astype(BF16)
    from_back = [None] + [send(back_out, back_in.at[e], tm=plus(e)) for e in range(1, NTM)]
    back_in[0] = back_out[...]

    adj = jnp.zeros((NBLK * ROWS, BLK), F32)
    for q in range(4):
        for e in range(4 * q, 4 * q + 4):
            if e:
                from_back[e].wait_recv()
        adj += nn_dot(
            gt4[:, q * 4 * SLOTS : (q + 1) * 4 * SLOTS],
            back_in[4 * q : 4 * q + 4].reshape(4 * SLOTS, BLK),
        )
    for b in range(NBLK):
        adj_v[:, b * BLK : (b + 1) * BLK] = adj[b * ROWS : (b + 1) * ROWS, :].astype(BF16)

    def terms(rel, c, out):
        @pl.loop(0, COLS // BLK)
        def _(n):
            cols = pl.ds(pl.multiple_of(n * BLK, BLK), BLK)
            out[:, cols] = nn_dot(adj_v[...], space_v[rel, c, :, cols]).astype(out.dtype)

    from_pair = {}

    def to_sibling(rel):
        terms(rel, 1, sib_out.at[rel])
        from_pair[rel] = send(sib_out.at[rel], sib_in.at[rel], space=sibling)

    def pair(rel, rows):
        return term_v[rel, rows, :] + sib_in[rel, rows, :].astype(F32)

    to_sibling(OPP)
    terms(OPP, 0, term_v.at[OPP])
    to_sibling(LEFT)
    from_pair[OPP].wait_recv()
    hop_out[0] = pair(OPP, top).astype(BF16)
    far_left = send(hop_out.at[0], hop_in.at[0], space=right)
    hop_out[1] = pair(OPP, low).astype(BF16)
    far_right = send(hop_out.at[1], hop_in.at[1], space=left)
    to_sibling(RIGHT)
    terms(LEFT, 0, term_v.at[LEFT])
    from_pair[LEFT].wait_recv()
    hop_out[2] = pair(LEFT, top).astype(BF16)
    near_right = send(hop_out.at[2], hop_in.at[2], space=left)
    terms(RIGHT, 0, term_v.at[RIGHT])
    from_pair[RIGHT].wait_recv()
    hop_out[3] = pair(RIGHT, low).astype(BF16)
    near_left = send(hop_out.at[3], hop_in.at[3], space=right)
    to_sibling(OWN)
    far_left.wait_recv()
    hop_out[4] = (pair(RIGHT, top) + hop_in[0].astype(F32)).astype(BF16)
    last_left = send(hop_out.at[4], hop_in.at[4], space=right)
    far_right.wait_recv()
    hop_out[5] = (pair(LEFT, low) + hop_in[1].astype(F32)).astype(BF16)
    last_right = send(hop_out.at[5], hop_in.at[5], space=left)
    terms(OWN, 0, term_v.at[OWN])
    from_pair[OWN].wait_recv()
    out_v[...] = state_v[...] + term_v[OWN] + sib_in[OWN].astype(F32)
    near_right.wait_recv()
    out_v[top, :] += hop_in[2].astype(F32)
    near_left.wait_recv()
    out_v[low, :] += hop_in[3].astype(F32)
    last_left.wait_recv()
    out_v[top, :] += hop_in[4].astype(F32)
    out0 = pltpu.make_async_copy(out_v.at[top], out_hbm.at[top], lsem.at[len(loads)])
    out0.start()
    last_right.wait_recv()
    out_v[low, :] += hop_in[5].astype(F32)
    out1 = pltpu.make_async_copy(out_v.at[low], out_hbm.at[low], lsem.at[len(loads) + 1])
    out1.start()
    for copy in sends:
        copy.wait_send()
    out0.wait()
    out1.wait()


N_LOADS = 18
N_SENDS = 15 + 6 + 7 + 15 + 7 + 15 + 4 + 6


def local(
    state,
    space_factor,
    time_factor,
    footprints,
    tile_obs,
    tile_block,
    tile_time,
    tile_count,
    obs_dep,
    obs_weight,
):
    any_spec = pl.BlockSpec(memory_space=pl.ANY)
    vm = pltpu.VMEM
    return pl.pallas_call(
        kernel,
        out_shape=jax.ShapeDtypeStruct((ROWS, COLS), F32),
        in_specs=[any_spec] * 10,
        out_specs=any_spec,
        scratch_shapes=[
            vm((ROWS, COLS), F32),
            vm((NX, 2, COLS, COLS), BF16),
            vm((TIMES, ROWS), F32),
            vm((SLOTS, OBS, BLK), BF16),
            vm((1, SLOTS), jnp.int32),
            vm((1, SLOTS), jnp.int32),
            vm((1, SLOTS), jnp.int32),
            vm((1, 1), jnp.int32),
            vm((SLOTS, OBS), F32),
            vm((SLOTS, OBS), F32),
            vm((ROWS, COLS), F32),
            vm((NX, 2, ROWS, COLS), BF16),
            vm((ROWS, COLS), F32),
            vm((ROWS, TIMES), BF16),
            vm((2, 8, 2 * SLOTS), jnp.int32),
            vm((NTM, 8, 2 * SLOTS), jnp.int32),
            vm((NBLK * ROWS, NTM * SLOTS), BF16),
            vm((NTM * SLOTS, NBLK * ROWS), BF16),
            vm((NTM, SLOTS, BLK), BF16),
            vm((NTM, SLOTS, BLK), BF16),
            vm((SLOTS, OBS), F32),
            vm((SLOTS, OBS), BF16),
            vm((NSP, SLOTS, OBS), BF16),
            vm((SLOTS, BLK), BF16),
            vm((NTM, SLOTS, BLK), BF16),
            vm((ROWS, COLS), BF16),
            vm((NX, ROWS, COLS), BF16),
            vm((NX, ROWS, COLS), BF16),
            vm((NX, ROWS, COLS), F32),
            vm((6, HALF, COLS), BF16),
            vm((6, HALF, COLS), BF16),
            pltpu.SemaphoreType.DMA((N_LOADS + 2,)),
            pltpu.SemaphoreType.DMA((N_SENDS,)),
            pltpu.SemaphoreType.DMA((N_SENDS,)),
        ],
        compiler_params=pltpu.CompilerParams(
            collective_id=0, has_side_effects=True, vmem_limit_bytes=56 * 1024 * 1024
        ),
    )(
        state,
        space_factor,
        time_factor,
        footprints.reshape(SLOTS, OBS, BLK),
        tile_obs.reshape(1, SLOTS),
        tile_block.reshape(1, SLOTS),
        tile_time.reshape(1, SLOTS),
        tile_count,
        obs_dep,
        obs_weight,
    )


def solution(mesh):
    return jax.shard_map(
        local,
        mesh=mesh,
        in_specs=(
            P("tm", "space"),
            P("space", None),
            P(),
            P("tm", "space", None, None),
            P("tm", "space"),
            P("tm", "space"),
            P("tm", "space"),
            P("tm", "space"),
            P("tm", None),
            P("tm", None),
        ),
        out_specs=P("tm", "space"),
        check_vma=False,
    )
```

```python
import functools

import jax
import jax.numpy as jnp
from jax import lax
from jax.experimental import pallas as pl
from jax.experimental.pallas import tpu as pltpu
from jax.sharding import PartitionSpec as P

MESH = pl.DeviceIdType.MESH
F32 = jnp.float32
BF16 = jnp.bfloat16
NX = 4
NTM = 16
NSP = 8
SLOTS = 64
ROWS = 128
COLS = 1024
HALF = COLS // 2
BLK = 256
NBLK = COLS // BLK
OBS = 128
TIMES = 2048
OWN, RIGHT, OPP, LEFT = 0, 1, 2, 3


FAR_FIRST = (10, 11, 6, 9, 14, 2, 8, 7, 5, 13, 15, 3, 1, 12, 4)


def nt_dot(a, b):
    return lax.dot_general(a, b, (((1,), (1,)), ((), ())), preferred_element_type=F32)


def nn_dot(a, b):
    return jnp.dot(a, b, preferred_element_type=F32)


def kernel(
    state_hbm,
    space_hbm,
    time_hbm,
    foot_hbm,
    obs_hbm,
    block_hbm,
    when_hbm,
    count_hbm,
    dep_hbm,
    weight_hbm,
    out_hbm,
    state_v,
    space_v,
    time_v,
    foot_v,
    foot_t,
    obs_v,
    block_v,
    when_v,
    count_v,
    dep_v,
    weight_v,
    out_v,
    xall,
    spread_v,
    time_t,
    meta_out,
    meta_y,
    line_out,
    meta_z,
    gt,
    gt4,
    g4,
    part_out,
    part_in,
    sims_v,
    evo_out,
    evo_in,
    back_out,
    back_in,
    adj_v,
    sib_out,
    sib_in,
    term_v,
    hop_out,
    hop_in,
    lsem,
    ssem,
    rsem,
):
    tm = lax.axis_index("tm")
    sp = lax.axis_index("space")
    z, y = lax.div(tm, NX), lax.rem(tm, NX)
    x, core = lax.div(sp, 2), lax.rem(sp, 2)
    other = 1 - core

    def at_x(rel, c):
        return lax.rem(x + rel, NX) * 2 + (other if c else core)

    def plus(e):
        dz, dy = divmod(e, NX)
        return lax.rem(z + dz, NX) * NX + lax.rem(y + dy, NX)

    def minus(e):
        dz, dy = divmod(e, NX)
        return lax.rem(z + NX - dz, NX) * NX + lax.rem(y + NX - dy, NX)

    loads = []

    def load(src, dst):
        copy = pltpu.make_async_copy(src, dst, lsem.at[len(loads)])
        copy.start()
        loads.append(copy)
        return copy

    sends = []

    def send(src, dst, **where):
        n = len(sends)
        copy = pltpu.make_async_remote_copy(
            src_ref=src,
            dst_ref=dst,
            send_sem=ssem.at[n],
            recv_sem=rsem.at[n],
            device_id=where,
            device_id_type=MESH,
        )
        copy.start()
        sends.append(copy)
        return copy

    right, left = at_x(RIGHT, 0), at_x(LEFT, 0)
    sibling = at_x(OWN, 1)

    ld_state = load(state_hbm, state_v)
    ld_when = load(when_hbm, when_v)
    ld_block = load(block_hbm, block_v)
    ld_count = load(count_hbm, count_v)
    barrier = pltpu.get_barrier_semaphore()
    for d in (sibling, right, left):
        pl.semaphore_signal(barrier, inc=1, device_id={"space": d}, device_id_type=MESH)
    for e in (2, 1, 3, 2 * NX, NX, 3 * NX):
        pl.semaphore_signal(barrier, inc=1, device_id={"tm": plus(e)}, device_id_type=MESH)

    ld_state.wait()
    ld_space = {}

    def load_space(rel, c):
        cols = pl.ds(pl.multiple_of(at_x(rel, c) * COLS, COLS), COLS)
        ld_space[rel, c] = load(space_hbm.at[:, cols], space_v.at[rel, c])

    load_space(OWN, 0)
    load_space(OWN, 1)
    ld_time = load(time_hbm.at[:, pl.ds(pl.multiple_of(tm * ROWS, ROWS), ROWS)], time_v)
    for rel in (LEFT, RIGHT, OPP):
        load_space(rel, 0)
        load_space(rel, 1)
    ld_foot = load(foot_hbm, foot_v)
    ld_obs = load(obs_hbm, obs_v)
    ld_dep = load(dep_hbm, dep_v)
    ld_weight = load(weight_hbm, weight_v)

    for h in range(2):
        xall[OWN, 0, h] = state_v[:, h * HALF : (h + 1) * HALF].astype(BF16)
    ld_when.wait()
    ld_block.wait()
    ld_count.wait()
    lane = lax.broadcasted_iota(jnp.int32, (1, SLOTS), 1)
    code = when_v[...] * 8 + (block_v[...] - sp * NBLK)
    code = jnp.where(lane < count_v[...], code, -8)
    zero = jnp.zeros((1, SLOTS), jnp.int32)
    meta_out[0] = jnp.broadcast_to(jnp.concatenate([code, zero], axis=1), (8, 2 * SLOTS))
    meta_out[1] = jnp.broadcast_to(jnp.concatenate([zero, code], axis=1), (8, 2 * SLOTS))
    pl.semaphore_wait(barrier, 9)

    def block_to(rel, at, h, where):
        return send(xall.at[rel, 0, h], xall.at[at, 0, h], space=where)

    def block_over(rel, h):
        return send(xall.at[rel, 0, h], xall.at[rel, 1, h], space=sibling)

    got = {}
    got[LEFT, 0, 0] = block_to(OWN, LEFT, 0, right)
    got[RIGHT, 0, 1] = block_to(OWN, RIGHT, 1, left)
    from_y = [None] + [send(meta_out.at[d % 2], meta_y.at[d], tm=plus(d)) for d in range(1, NX)]
    got[LEFT, 0, 1] = block_to(OWN, LEFT, 1, right)
    got[RIGHT, 0, 0] = block_to(OWN, RIGHT, 0, left)
    for h in range(2):
        got[OWN, 1, h] = block_over(OWN, h)

    def add_spread(rel, c, h, first=False):
        term = nt_dot(xall[rel, c, h], space_v[rel, c, :, h * HALF : (h + 1) * HALF])
        if first:
            spread_v[...] = term
        else:
            spread_v[...] += term

    ld_space[OWN, 0].wait()
    add_spread(OWN, 0, 0, first=True)
    add_spread(OWN, 0, 1)
    for d in range(1, NX):
        from_y[d].wait_recv()
    line_out[0] = meta_out[0] + meta_y[1]
    line_out[1] = meta_y[2] + meta_y[3]
    from_z = [None] + [send(line_out, meta_z.at[d], tm=plus(d * NX)) for d in range(1, NX)]
    meta_z[0] = line_out[...]
    ld_space[OWN, 1].wait()
    for h in range(2):
        got[OWN, 1, h].wait_recv()
        add_spread(OWN, 1, h)
    ld_time.wait()
    time_t[...] = time_v[...].T.astype(BF16)
    got[LEFT, 0, 0].wait_recv()
    got[OPP, 0, 0] = block_to(LEFT, OPP, 0, right)
    got[RIGHT, 0, 1].wait_recv()
    got[OPP, 0, 1] = block_to(RIGHT, OPP, 1, left)
    got[LEFT, 1, 0] = block_over(LEFT, 0)
    got[RIGHT, 1, 1] = block_over(RIGHT, 1)

    for d in range(1, NX):
        from_z[d].wait_recv()

    @pl.loop(0, NX)
    def _(d):
        row = jnp.concatenate([meta_z[d, 0, 0:1, :], meta_z[d, 1, 0:1, :]], axis=1)
        when = lax.shift_right_arithmetic(row, 3)
        which = jnp.bitwise_and(row, 7)
        hot = lax.broadcasted_iota(jnp.int32, (TIMES, NX * SLOTS), 0) == when
        picked = nn_dot(time_t[...], jnp.where(hot, 1.0, 0.0).astype(BF16))
        slots = pl.ds(pl.multiple_of(d * NX * SLOTS, NX * SLOTS), NX * SLOTS)
        gt[:, slots] = picked.astype(BF16)
        picked_t = picked.T
        which_t = jnp.broadcast_to(which.astype(F32), (ROWS, NX * SLOTS)).T
        for b in range(NBLK):
            g4[slots, b * ROWS : (b + 1) * ROWS] = jnp.where(
                which_t == float(b), picked_t, 0.0
            ).astype(BF16)

    for rel, c, h in ((LEFT, 0, 0), (RIGHT, 0, 1), (LEFT, 1, 0), (RIGHT, 1, 1)):
        if h == (rel == RIGHT) and c == 0:
            ld_space[rel, 0].wait()
            ld_space[rel, 1].wait()
        if c:
            got[rel, c, h].wait_recv()
        add_spread(rel, c, h)
    for rel, h in ((LEFT, 1), (RIGHT, 0)):
        got[rel, 0, h].wait_recv()
        got[rel, 1, h] = block_over(rel, h)
    for rel, h in ((LEFT, 1), (RIGHT, 0)):
        add_spread(rel, 0, h)
    for rel, h in ((LEFT, 1), (RIGHT, 0)):
        got[rel, 1, h].wait_recv()
        add_spread(rel, 1, h)
    ld_space[OPP, 0].wait()
    ld_space[OPP, 1].wait()
    for h in range(2):
        got[OPP, 0, h].wait_recv()
        got[OPP, 1, h] = block_over(OPP, h)
    for c in range(2):
        for h in range(2):
            if c:
                got[OPP, 1, h].wait_recv()
            add_spread(OPP, c, h)

    spread4 = jnp.concatenate(
        [spread_v[:, b * BLK : (b + 1) * BLK].astype(BF16) for b in range(NBLK)], axis=0
    )
    from_part = [None] * NTM
    done = set()
    for e in FAR_FIRST + (0,):
        m = e // 2
        if m not in done:
            done.add(m)
            part = nn_dot(g4[m * 2 * SLOTS : (m + 1) * 2 * SLOTS, :], spread4)
            part_out[2 * m : 2 * m + 2] = part.astype(BF16).reshape(2, SLOTS, BLK)
        if e:
            from_part[e] = send(part_out.at[e], part_in.at[e], tm=minus(e))

    for b in range(NBLK):
        for d in range(NX):
            which = jnp.bitwise_and(
                jnp.concatenate([meta_z[d, 0, 0:1, :], meta_z[d, 1, 0:1, :]], axis=1), 7
            )
            slots = slice(d * NX * SLOTS, (d + 1) * NX * SLOTS)
            gt4[b * ROWS : (b + 1) * ROWS, slots] = jnp.where(
                which == b, gt[:, slots].astype(F32), 0.0
            ).astype(BF16)
    ld_foot.wait()

    @pl.loop(0, SLOTS // 4)
    def _(k):
        for i in range(4):
            foot_t[4 * k + i] = foot_v[4 * k + i].T

    ld_obs.wait()
    pick = jnp.where(
        lax.broadcasted_iota(jnp.int32, (SLOTS, SLOTS), 0) == obs_v[...] - tm * SLOTS, 1.0, 0.0
    )
    pick_low = pick.astype(BF16)
    pick_t = pick.T.astype(BF16)
    ld_dep.wait()
    ld_weight.wait()

    flux = part_out[0].astype(F32)
    for e in FAR_FIRST[::-1]:
        from_part[e].wait_recv()
        flux += part_in[e].astype(F32)
    flux = flux.astype(BF16)

    group = 16
    row16 = lax.broadcasted_iota(jnp.int32, (group, BLK), 0)
    for g in range(SLOTS // group):
        mine = flux[g * group : (g + 1) * group, :]
        acc = jnp.zeros((group, OBS), F32)
        for k in range(group):
            acc += nn_dot(jnp.where(row16 == k, mine, jnp.zeros_like(mine)), foot_t[g * group + k])
        sims_v[g * group : (g + 1) * group, :] = acc
    sims = sims_v[...]
    sims_hi = sims.astype(BF16)
    sims_lo = (sims - sims_hi.astype(F32)).astype(BF16)
    evolved = nn_dot(pick_low, sims_hi) + nn_dot(pick_low, sims_lo)
    evo_out[...] = evolved.astype(BF16)
    from_evo = []
    for rel, c in ((OPP, 1), (OPP, 0), (RIGHT, 1), (LEFT, 1), (RIGHT, 0), (LEFT, 0), (OWN, 1)):
        from_evo.append(send(evo_out, evo_in.at[len(from_evo)], space=at_x(rel, c)))
    for n in range(NSP - 1)[::-1]:
        from_evo[n].wait_recv()
        evolved += evo_in[n].astype(F32)
    depart = (weight_v[...] * (evolved - dep_v[...])).astype(BF16)
    mine_dep = nn_dot(pick_t, depart).astype(BF16)

    row16 = lax.broadcasted_iota(jnp.int32, (group, OBS), 0)
    for g in range(SLOTS // group):
        mine = mine_dep[g * group : (g + 1) * group, :]
        acc = jnp.zeros((group, BLK), F32)
        for k in range(group):
            acc += nn_dot(jnp.where(row16 == k, mine, jnp.zeros_like(mine)), foot_v[g * group + k])
        back_out[g * group : (g + 1) * group, :] = acc.astype(BF16)
    from_back = [None] * NTM
    for e in FAR_FIRST:
        from_back[e] = send(back_out, back_in.at[e], tm=plus(e))
    back_in[0] = back_out[...]

    adj = jnp.zeros((NBLK * ROWS, BLK), F32)
    for q in (0, 1, 3, 2):
        for e in range(4 * q, 4 * q + 4):
            if e:
                from_back[e].wait_recv()
        adj += nn_dot(
            gt4[:, q * 4 * SLOTS : (q + 1) * 4 * SLOTS],
            back_in[4 * q : 4 * q + 4].reshape(4 * SLOTS, BLK),
        )
    for b in range(NBLK):
        adj_v[:, b * BLK : (b + 1) * BLK] = adj[b * ROWS : (b + 1) * ROWS, :].astype(BF16)

    def terms(rel, c, h):
        return nn_dot(adj_v[...], space_v[rel, c, :, h * HALF : (h + 1) * HALF])

    from_pair = {}

    def to_sibling(rel, h):
        sib_out[rel, h] = terms(rel, 1, h).astype(BF16)
        from_pair[rel, h] = send(sib_out.at[rel, h], sib_in.at[rel, h], space=sibling)

    def own_terms(rel, h):
        term_v[rel, h] = terms(rel, 0, h)

    def pair(rel, h):
        from_pair[rel, h].wait_recv()
        return term_v[rel, h] + sib_in[rel, h].astype(F32)

    def hop(n, value, where):
        hop_out[n] = value.astype(BF16)
        return send(hop_out.at[n], hop_in.at[n], space=where)

    to_sibling(OPP, 0)
    to_sibling(OPP, 1)
    own_terms(OPP, 0)
    own_terms(OPP, 1)
    to_sibling(LEFT, 0)
    to_sibling(RIGHT, 1)
    far_left = hop(0, pair(OPP, 0), right)
    far_right = hop(1, pair(OPP, 1), left)
    own_terms(LEFT, 0)
    own_terms(RIGHT, 1)
    near_right = hop(2, pair(LEFT, 0), left)
    near_left = hop(3, pair(RIGHT, 1), right)
    to_sibling(RIGHT, 0)
    to_sibling(LEFT, 1)
    own_terms(RIGHT, 0)
    own_terms(LEFT, 1)
    term_v[RIGHT, 0] = pair(RIGHT, 0)
    term_v[LEFT, 1] = pair(LEFT, 1)
    far_left.wait_recv()
    last_left = hop(4, term_v[RIGHT, 0] + hop_in[0].astype(F32), right)
    far_right.wait_recv()
    last_right = hop(5, term_v[LEFT, 1] + hop_in[1].astype(F32), left)
    to_sibling(OWN, 0)
    to_sibling(OWN, 1)
    own_terms(OWN, 0)
    own_terms(OWN, 1)
    for h in range(2):
        cols = slice(h * HALF, (h + 1) * HALF)
        out_v[:, cols] = state_v[:, cols] + pair(OWN, h)
    near_right.wait_recv()
    out_v[:, :HALF] += hop_in[2].astype(F32)
    near_left.wait_recv()
    out_v[:, HALF:] += hop_in[3].astype(F32)
    outs = []
    for h, copy in enumerate((last_left, last_right)):
        cols = slice(h * HALF, (h + 1) * HALF)
        copy.wait_recv()
        out_v[:, cols] += hop_in[4 + h].astype(F32)
        outs.append(load(out_v.at[:, cols], out_hbm.at[:, cols]))
    for copy in sends:
        copy.wait_send()
    for copy in outs:
        copy.wait()


N_LOADS = 20
N_SENDS = 3 + 3 + 6 + 8 + 15 + 7 + 15 + 8 + 6


def local(
    state,
    space_factor,
    time_factor,
    footprints,
    tile_obs,
    tile_block,
    tile_time,
    tile_count,
    obs_dep,
    obs_weight,
):
    any_spec = pl.BlockSpec(memory_space=pl.ANY)
    vm = pltpu.VMEM
    i32 = jnp.int32
    return pl.pallas_call(
        kernel,
        out_shape=jax.ShapeDtypeStruct((ROWS, COLS), F32),
        in_specs=[any_spec] * 10,
        out_specs=any_spec,
        scratch_shapes=[
            vm((ROWS, COLS), F32),
            vm((NX, 2, COLS, COLS), BF16),
            vm((TIMES, ROWS), F32),
            vm((SLOTS, OBS, BLK), BF16),
            vm((SLOTS, BLK, OBS), BF16),
            vm((1, SLOTS), i32),
            vm((1, SLOTS), i32),
            vm((1, SLOTS), i32),
            vm((1, 1), i32),
            vm((SLOTS, OBS), F32),
            vm((SLOTS, OBS), F32),
            vm((ROWS, COLS), F32),
            vm((NX, 2, 2, ROWS, HALF), BF16),
            vm((ROWS, COLS), F32),
            vm((ROWS, TIMES), BF16),
            vm((2, 8, 2 * SLOTS), i32),
            vm((NX, 8, 2 * SLOTS), i32),
            vm((2, 8, 2 * SLOTS), i32),
            vm((NX, 2, 8, 2 * SLOTS), i32),
            vm((ROWS, NTM * SLOTS), BF16),
            vm((NBLK * ROWS, NTM * SLOTS), BF16),
            vm((NTM * SLOTS, NBLK * ROWS), BF16),
            vm((NTM, SLOTS, BLK), BF16),
            vm((NTM, SLOTS, BLK), BF16),
            vm((SLOTS, OBS), F32),
            vm((SLOTS, OBS), BF16),
            vm((NSP - 1, SLOTS, OBS), BF16),
            vm((SLOTS, BLK), BF16),
            vm((NTM, SLOTS, BLK), BF16),
            vm((ROWS, COLS), BF16),
            vm((NX, 2, ROWS, HALF), BF16),
            vm((NX, 2, ROWS, HALF), BF16),
            vm((NX, 2, ROWS, HALF), F32),
            vm((6, ROWS, HALF), BF16),
            vm((6, ROWS, HALF), BF16),
            pltpu.SemaphoreType.DMA((N_LOADS,)),
            pltpu.SemaphoreType.DMA((N_SENDS,)),
            pltpu.SemaphoreType.DMA((N_SENDS,)),
        ],
        compiler_params=pltpu.CompilerParams(
            collective_id=0, has_side_effects=True, vmem_limit_bytes=56 * 1024 * 1024
        ),
    )(
        state,
        space_factor,
        time_factor,
        footprints.reshape(SLOTS, OBS, BLK),
        tile_obs.reshape(1, SLOTS),
        tile_block.reshape(1, SLOTS),
        tile_time.reshape(1, SLOTS),
        tile_count,
        obs_dep,
        obs_weight,
    )


def solution(mesh):
    return jax.shard_map(
        local,
        mesh=mesh,
        in_specs=(
            P("tm", "space"),
            P("space", None),
            P(),
            P("tm", "space", None, None),
            P("tm", "space"),
            P("tm", "space"),
            P("tm", "space"),
            P("tm", "space"),
            P("tm", None),
            P("tm", None),
        ),
        out_specs=P("tm", "space"),
        check_vma=False,
    )
```

```python
import functools

import jax
import jax.numpy as jnp
from jax import lax
from jax.experimental import pallas as pl
from jax.experimental.pallas import tpu as pltpu
from jax.sharding import PartitionSpec as P

MESH = pl.DeviceIdType.MESH
F32 = jnp.float32
BF16 = jnp.bfloat16
NX = 4
NTM = 16
NSP = 8
SLOTS = 64
ROWS = 128
COLS = 1024
HALF = COLS // 2
BLK = 256
NBLK = COLS // BLK
OBS = 128
TIMES = 2048
OWN, RIGHT, OPP, LEFT = 0, 1, 2, 3


FAR_FIRST = (10, 11, 6, 9, 14, 2, 8, 7, 5, 13, 15, 3, 1, 12, 4)


def nt_dot(a, b):
    return lax.dot_general(a, b, (((1,), (1,)), ((), ())), preferred_element_type=F32)


def nn_dot(a, b):
    return jnp.dot(a, b, preferred_element_type=F32)


def kernel(
    state_hbm,
    space_hbm,
    time_hbm,
    foot_hbm,
    obs_hbm,
    block_hbm,
    when_hbm,
    count_hbm,
    dep_hbm,
    weight_hbm,
    out_v,
    state_v,
    space_v,
    time_v,
    foot_v,
    foot_t,
    obs_v,
    block_v,
    when_v,
    count_v,
    dep_v,
    weight_v,
    xall,
    spread_v,
    time_t,
    meta_out,
    meta_y,
    line_out,
    meta_z,
    gt,
    gt4,
    g4,
    part_out,
    part_in,
    sims_v,
    evo_out,
    evo_in,
    back_out,
    back_in,
    adj_v,
    sib_out,
    sib_in,
    term_v,
    hop_out,
    hop_in,
    lsem,
    ssem,
    rsem,
    bssem,
    brsem,
):
    tm = lax.axis_index("tm")
    sp = lax.axis_index("space")
    z, y = lax.div(tm, NX), lax.rem(tm, NX)
    x, core = lax.div(sp, 2), lax.rem(sp, 2)
    other = 1 - core

    def at_x(rel, c):
        return lax.rem(x + rel, NX) * 2 + (other if c else core)

    def plus(e):
        dz, dy = divmod(e, NX)
        return lax.rem(z + dz, NX) * NX + lax.rem(y + dy, NX)

    def minus(e):
        dz, dy = divmod(e, NX)
        return lax.rem(z + NX - dz, NX) * NX + lax.rem(y + NX - dy, NX)

    loads = []

    def load(src, dst):
        copy = pltpu.make_async_copy(src, dst, lsem.at[len(loads)])
        copy.start()
        loads.append(copy)
        return copy

    sends = []

    def send(src, dst, **where):
        n = len(sends)
        copy = pltpu.make_async_remote_copy(
            src_ref=src,
            dst_ref=dst,
            send_sem=ssem.at[n],
            recv_sem=rsem.at[n],
            device_id=where,
            device_id_type=MESH,
        )
        copy.start()
        sends.append(copy)
        return copy

    right, left = at_x(RIGHT, 0), at_x(LEFT, 0)
    sibling = at_x(OWN, 1)

    ld_state = load(state_hbm, state_v)
    ld_when = load(when_hbm, when_v)
    ld_block = load(block_hbm, block_v)
    ld_count = load(count_hbm, count_v)
    barrier = pltpu.get_barrier_semaphore()
    for d in (sibling, right, left):
        pl.semaphore_signal(barrier, inc=1, device_id={"space": d}, device_id_type=MESH)
    for e in (2, 1, 3, 2 * NX, NX, 3 * NX):
        pl.semaphore_signal(barrier, inc=1, device_id={"tm": plus(e)}, device_id_type=MESH)

    ld_state.wait()
    ld_space = {}

    def load_space(rel, c):
        cols = pl.ds(pl.multiple_of(at_x(rel, c) * COLS, COLS), COLS)
        ld_space[rel, c] = load(space_hbm.at[:, cols], space_v.at[rel, c])

    load_space(OWN, 0)
    load_space(OWN, 1)
    ld_time = load(time_hbm.at[:, pl.ds(pl.multiple_of(tm * ROWS, ROWS), ROWS)], time_v)
    for rel in (LEFT, RIGHT, OPP):
        load_space(rel, 0)
        load_space(rel, 1)
    ld_foot = load(foot_hbm, foot_v)
    ld_obs = load(obs_hbm, obs_v)
    ld_dep = load(dep_hbm, dep_v)
    ld_weight = load(weight_hbm, weight_v)

    for h in range(2):
        xall[OWN, 0, h] = state_v[:, h * HALF : (h + 1) * HALF].astype(BF16)
    ld_when.wait()
    ld_block.wait()
    ld_count.wait()
    lane = lax.broadcasted_iota(jnp.int32, (1, SLOTS), 1)
    code = when_v[...] * 8 + (block_v[...] - sp * NBLK)
    code = jnp.where(lane < count_v[...], code, -8)
    zero = jnp.zeros((1, SLOTS), jnp.int32)
    meta_out[0] = jnp.broadcast_to(jnp.concatenate([code, zero], axis=1), (8, 2 * SLOTS))
    meta_out[1] = jnp.broadcast_to(jnp.concatenate([zero, code], axis=1), (8, 2 * SLOTS))
    pl.semaphore_wait(barrier, 9)

    def block_to(rel, at, h, where):
        return send(xall.at[rel, 0, h], xall.at[at, 0, h], space=where)

    def block_over(rel, h):
        return send(xall.at[rel, 0, h], xall.at[rel, 1, h], space=sibling)

    got = {}
    got[LEFT, 0, 0] = block_to(OWN, LEFT, 0, right)
    got[RIGHT, 0, 1] = block_to(OWN, RIGHT, 1, left)
    odd = lax.rem(y, 2)
    from_y = [None] + [send(meta_out.at[odd], meta_y.at[y], tm=plus(d)) for d in range(1, NX)]
    meta_y[y] = meta_out[odd]
    got[LEFT, 0, 1] = block_to(OWN, LEFT, 1, right)
    got[RIGHT, 0, 0] = block_to(OWN, RIGHT, 0, left)
    for h in range(2):
        got[OWN, 1, h] = block_over(OWN, h)

    def add_spread(rel, c, h, first=False):
        term = nt_dot(xall[rel, c, h], space_v[rel, c, :, h * HALF : (h + 1) * HALF])
        if first:
            spread_v[...] = term
        else:
            spread_v[...] += term

    ld_space[OWN, 0].wait()
    add_spread(OWN, 0, 0, first=True)
    add_spread(OWN, 0, 1)
    for d in range(1, NX):
        from_y[d].wait_recv()
    line_out[0] = meta_y[0] + meta_y[1]
    line_out[1] = meta_y[2] + meta_y[3]
    from_z = [None] + [send(line_out, meta_z.at[z], tm=plus(d * NX)) for d in range(1, NX)]
    meta_z[z] = line_out[...]
    ld_space[OWN, 1].wait()
    for h in range(2):
        got[OWN, 1, h].wait_recv()
        add_spread(OWN, 1, h)
    ld_time.wait()
    time_t[...] = time_v[...].T.astype(BF16)
    got[LEFT, 0, 0].wait_recv()
    got[OPP, 0, 0] = block_to(LEFT, OPP, 0, right)
    got[RIGHT, 0, 1].wait_recv()
    got[OPP, 0, 1] = block_to(RIGHT, OPP, 1, left)
    got[LEFT, 1, 0] = block_over(LEFT, 0)
    got[RIGHT, 1, 1] = block_over(RIGHT, 1)

    for rel, h in ((LEFT, 0), (RIGHT, 1)):
        ld_space[rel, 0].wait()
        add_spread(rel, 0, h)
    for rel, h in ((LEFT, 1), (RIGHT, 0)):
        got[rel, 0, h].wait_recv()
        got[rel, 1, h] = block_over(rel, h)
    for rel, h in ((LEFT, 0), (RIGHT, 1)):
        ld_space[rel, 1].wait()
        got[rel, 1, h].wait_recv()
        add_spread(rel, 1, h)
    for rel, h in ((LEFT, 1), (RIGHT, 0)):
        add_spread(rel, 0, h)

    for d in range(1, NX):
        from_z[d].wait_recv()

    for d in range(NX):
        row = jnp.concatenate([meta_z[d, 0, 0:1, :], meta_z[d, 1, 0:1, :]], axis=1)
        when = lax.shift_right_arithmetic(row, 3)
        which = jnp.bitwise_and(row, 7)
        hot = lax.broadcasted_iota(jnp.int32, (TIMES, NX * SLOTS), 0) == when
        picked = nn_dot(time_t[...], jnp.where(hot, 1.0, 0.0).astype(BF16))
        slots = slice(d * NX * SLOTS, (d + 1) * NX * SLOTS)
        gt[:, slots] = picked.astype(BF16)
        picked_t = picked.T
        which_t = jnp.broadcast_to(which.astype(F32), (ROWS, NX * SLOTS)).T
        for b in range(NBLK):
            g4[slots, b * ROWS : (b + 1) * ROWS] = jnp.where(
                which_t == float(b), picked_t, 0.0
            ).astype(BF16)

    for h in range(2):
        got[OPP, 0, h].wait_recv()
        got[OPP, 1, h] = block_over(OPP, h)
    for rel, h in ((LEFT, 1), (RIGHT, 0)):
        got[rel, 1, h].wait_recv()
        add_spread(rel, 1, h)
    for c in range(2):
        ld_space[OPP, c].wait()
        for h in range(2):
            if c:
                got[OPP, 1, h].wait_recv()
            add_spread(OPP, c, h)

    spread4 = jnp.concatenate(
        [spread_v[:, b * BLK : (b + 1) * BLK].astype(BF16) for b in range(NBLK)], axis=0
    )
    for m in range(NTM // 2):
        part = nn_dot(g4[m * 2 * SLOTS : (m + 1) * 2 * SLOTS, :], spread4)
        part_out[2 * m : 2 * m + 2] = part.astype(BF16).reshape(2, SLOTS, BLK)
    from_part = [None] * NTM
    for e in FAR_FIRST:
        from_part[e] = send(part_out.at[minus(e)], part_in.at[e], tm=minus(e))

    for b in range(NBLK):
        for d in range(NX):
            which = jnp.bitwise_and(
                jnp.concatenate([meta_z[d, 0, 0:1, :], meta_z[d, 1, 0:1, :]], axis=1), 7
            )
            slots = slice(d * NX * SLOTS, (d + 1) * NX * SLOTS)
            gt4[b * ROWS : (b + 1) * ROWS, slots] = jnp.where(
                which == b, gt[:, slots].astype(F32), 0.0
            ).astype(BF16)
    ld_foot.wait()

    @pl.loop(0, SLOTS // 4)
    def _(k):
        for i in range(4):
            foot_t[4 * k + i] = foot_v[4 * k + i].T

    ld_obs.wait()
    pick = jnp.where(
        lax.broadcasted_iota(jnp.int32, (SLOTS, SLOTS), 0) == obs_v[...] - tm * SLOTS, 1.0, 0.0
    )
    pick_low = pick.astype(BF16)
    pick_t = pick.T.astype(BF16)
    ld_dep.wait()
    ld_weight.wait()

    flux = part_out[tm].astype(F32)
    for e in FAR_FIRST[::-1]:
        from_part[e].wait_recv()
        flux += part_in[e].astype(F32)
    flux = flux.astype(BF16)

    group = 16
    row16 = lax.broadcasted_iota(jnp.int32, (group, BLK), 0)
    for g in range(SLOTS // group):
        mine = flux[g * group : (g + 1) * group, :]
        acc = jnp.zeros((group, OBS), F32)
        for k in range(group):
            acc += nn_dot(jnp.where(row16 == k, mine, jnp.zeros_like(mine)), foot_t[g * group + k])
        sims_v[g * group : (g + 1) * group, :] = acc
    sims = sims_v[...]
    sims_hi = sims.astype(BF16)
    sims_lo = (sims - sims_hi.astype(F32)).astype(BF16)
    evolved = nn_dot(pick_low, sims_hi) + nn_dot(pick_low, sims_lo)
    evo_out[...] = evolved.astype(BF16)
    from_evo = []
    for rel, c in ((OPP, 1), (OPP, 0), (RIGHT, 1), (LEFT, 1), (RIGHT, 0), (LEFT, 0), (OWN, 1)):
        from_evo.append(send(evo_out, evo_in.at[len(from_evo)], space=at_x(rel, c)))
    for n in range(NSP - 1)[::-1]:
        from_evo[n].wait_recv()
        evolved += evo_in[n].astype(F32)
    depart = (weight_v[...] * (evolved - dep_v[...])).astype(BF16)
    mine_dep = nn_dot(pick_t, depart).astype(BF16)

    row16 = lax.broadcasted_iota(jnp.int32, (group, OBS), 0)
    for g in range(SLOTS // group):
        mine = mine_dep[g * group : (g + 1) * group, :]
        acc = jnp.zeros((group, BLK), F32)
        for k in range(group):
            acc += nn_dot(jnp.where(row16 == k, mine, jnp.zeros_like(mine)), foot_v[g * group + k])
        back_out[g * group : (g + 1) * group, :] = acc.astype(BF16)
    def back_copy(dest, source):
        return pltpu.make_async_remote_copy(
            src_ref=back_out,
            dst_ref=back_in.at[source],
            send_sem=bssem.at[dest],
            recv_sem=brsem.at[source],
            device_id={"tm": dest},
            device_id_type=MESH,
        )

    for d in range(NTM):

        @pl.when(tm != d)
        def _(d=d):
            back_copy(d, tm).start()

    back_in[tm] = back_out[...]

    adj = jnp.zeros((NBLK * ROWS, BLK), F32)
    for q in range(4):
        for e in range(4 * q, 4 * q + 4):

            @pl.when(tm != e)
            def _(e=e):
                back_copy(e, e).wait_recv()

        adj += nn_dot(
            gt4[:, q * 4 * SLOTS : (q + 1) * 4 * SLOTS],
            back_in[4 * q : 4 * q + 4].reshape(4 * SLOTS, BLK),
        )
    for b in range(NBLK):
        adj_v[:, b * BLK : (b + 1) * BLK] = adj[b * ROWS : (b + 1) * ROWS, :].astype(BF16)

    def terms(rel, c, h):
        return nn_dot(adj_v[...], space_v[rel, c, :, h * HALF : (h + 1) * HALF])

    from_pair = {}

    def to_sibling(rel, h):
        sib_out[rel, h] = terms(rel, 1, h).astype(BF16)
        from_pair[rel, h] = send(sib_out.at[rel, h], sib_in.at[rel, h], space=sibling)

    def own_terms(rel, h):
        term_v[rel, h] = terms(rel, 0, h)

    def pair(rel, h):
        from_pair[rel, h].wait_recv()
        return term_v[rel, h] + sib_in[rel, h].astype(F32)

    def hop(n, value, where):
        hop_out[n] = value.astype(BF16)
        return send(hop_out.at[n], hop_in.at[n], space=where)

    to_sibling(OPP, 0)
    to_sibling(OPP, 1)
    own_terms(OPP, 0)
    own_terms(OPP, 1)
    to_sibling(LEFT, 0)
    to_sibling(RIGHT, 1)
    far_left = hop(0, pair(OPP, 0), right)
    far_right = hop(1, pair(OPP, 1), left)
    own_terms(LEFT, 0)
    own_terms(RIGHT, 1)
    near_right = hop(2, pair(LEFT, 0), left)
    near_left = hop(3, pair(RIGHT, 1), right)
    to_sibling(RIGHT, 0)
    to_sibling(LEFT, 1)
    own_terms(RIGHT, 0)
    own_terms(LEFT, 1)
    term_v[RIGHT, 0] = pair(RIGHT, 0)
    term_v[LEFT, 1] = pair(LEFT, 1)
    far_left.wait_recv()
    last_left = hop(4, term_v[RIGHT, 0] + hop_in[0].astype(F32), right)
    far_right.wait_recv()
    last_right = hop(5, term_v[LEFT, 1] + hop_in[1].astype(F32), left)
    to_sibling(OWN, 0)
    to_sibling(OWN, 1)
    own_terms(OWN, 0)
    own_terms(OWN, 1)
    for h in range(2):
        cols = slice(h * HALF, (h + 1) * HALF)
        out_v[:, cols] = state_v[:, cols] + pair(OWN, h)
    near_right.wait_recv()
    out_v[:, :HALF] += hop_in[2].astype(F32)
    near_left.wait_recv()
    out_v[:, HALF:] += hop_in[3].astype(F32)
    for h, copy in enumerate((last_left, last_right)):
        cols = slice(h * HALF, (h + 1) * HALF)
        copy.wait_recv()
        out_v[:, cols] += hop_in[4 + h].astype(F32)
    for copy in sends:
        copy.wait_send()
    for d in range(NTM):

        @pl.when(tm != d)
        def _(d=d):
            back_copy(d, tm).wait_send()


N_LOADS = 17
N_SENDS = 3 + 3 + 6 + 8 + 15 + 7 + 8 + 6


def local(
    state,
    space_factor,
    time_factor,
    footprints,
    tile_obs,
    tile_block,
    tile_time,
    tile_count,
    obs_dep,
    obs_weight,
):
    any_spec = pl.BlockSpec(memory_space=pl.ANY)
    vm = pltpu.VMEM
    i32 = jnp.int32
    return pl.pallas_call(
        kernel,
        out_shape=pltpu.VMEM((ROWS, COLS), F32),
        in_specs=[any_spec] * 10,
        out_specs=pl.BlockSpec(memory_space=pltpu.VMEM),
        scratch_shapes=[
            vm((ROWS, COLS), F32),
            vm((NX, 2, COLS, COLS), BF16),
            vm((TIMES, ROWS), F32),
            vm((SLOTS, OBS, BLK), BF16),
            vm((SLOTS, BLK, OBS), BF16),
            vm((1, SLOTS), i32),
            vm((1, SLOTS), i32),
            vm((1, SLOTS), i32),
            vm((1, 1), i32),
            vm((SLOTS, OBS), F32),
            vm((SLOTS, OBS), F32),
            vm((NX, 2, 2, ROWS, HALF), BF16),
            vm((ROWS, COLS), F32),
            vm((ROWS, TIMES), BF16),
            vm((2, 8, 2 * SLOTS), i32),
            vm((NX, 8, 2 * SLOTS), i32),
            vm((2, 8, 2 * SLOTS), i32),
            vm((NX, 2, 8, 2 * SLOTS), i32),
            vm((ROWS, NTM * SLOTS), BF16),
            vm((NBLK * ROWS, NTM * SLOTS), BF16),
            vm((NTM * SLOTS, NBLK * ROWS), BF16),
            vm((NTM, SLOTS, BLK), BF16),
            vm((NTM, SLOTS, BLK), BF16),
            vm((SLOTS, OBS), F32),
            vm((SLOTS, OBS), BF16),
            vm((NSP - 1, SLOTS, OBS), BF16),
            vm((SLOTS, BLK), BF16),
            vm((NTM, SLOTS, BLK), BF16),
            vm((ROWS, COLS), BF16),
            vm((NX, 2, ROWS, HALF), BF16),
            vm((NX, 2, ROWS, HALF), BF16),
            vm((NX, 2, ROWS, HALF), F32),
            vm((6, ROWS, HALF), BF16),
            vm((6, ROWS, HALF), BF16),
            pltpu.SemaphoreType.DMA((N_LOADS,)),
            pltpu.SemaphoreType.DMA((N_SENDS,)),
            pltpu.SemaphoreType.DMA((N_SENDS,)),
            pltpu.SemaphoreType.DMA((NTM,)),
            pltpu.SemaphoreType.DMA((NTM,)),
        ],
        compiler_params=pltpu.CompilerParams(
            collective_id=0, has_side_effects=True, vmem_limit_bytes=56 * 1024 * 1024
        ),
    )(
        state,
        space_factor,
        time_factor,
        footprints.reshape(SLOTS, OBS, BLK),
        tile_obs.reshape(1, SLOTS),
        tile_block.reshape(1, SLOTS),
        tile_time.reshape(1, SLOTS),
        tile_count,
        obs_dep,
        obs_weight,
    )


def solution(mesh):
    return jax.shard_map(
        local,
        mesh=mesh,
        in_specs=(
            P("tm", "space"),
            P("space", None),
            P(),
            P("tm", "space", None, None),
            P("tm", "space"),
            P("tm", "space"),
            P("tm", "space"),
            P("tm", "space"),
            P("tm", None),
            P("tm", None),
        ),
        out_specs=P("tm", "space"),
        check_vma=False,
    )
```

```python
import functools

import jax
import jax.numpy as jnp
from jax import lax
from jax.experimental import pallas as pl
from jax.experimental.pallas import tpu as pltpu
from jax.sharding import PartitionSpec as P

MESH = pl.DeviceIdType.MESH
F32 = jnp.float32
BF16 = jnp.bfloat16
NX = 4
NTM = 16
NSP = 8
SLOTS = 64
ROWS = 128
COLS = 1024
HALF = COLS // 2
BLK = 256
NBLK = COLS // BLK
OBS = 128
TIMES = 2048
OWN, RIGHT, OPP, LEFT = 0, 1, 2, 3


FAR_FIRST = (10, 11, 6, 9, 14, 2, 8, 7, 5, 13, 15, 3, 1, 12, 4)


def nt_dot(a, b):
    return lax.dot_general(a, b, (((1,), (1,)), ((), ())), preferred_element_type=F32)


def nn_dot(a, b):
    return jnp.dot(a, b, preferred_element_type=F32)


def kernel(
    state_hbm,
    space_hbm,
    time_hbm,
    foot_hbm,
    obs_hbm,
    block_hbm,
    when_hbm,
    count_hbm,
    dep_hbm,
    weight_hbm,
    out_v,
    state_v,
    space_v,
    space_t,
    time_v,
    foot_v,
    foot_t,
    obs_v,
    block_v,
    when_v,
    count_v,
    dep_v,
    weight_v,
    xall,
    spread_v,
    time_t,
    meta_out,
    meta_y,
    line_out,
    meta_z,
    gt,
    gt4,
    g4,
    part_out,
    part_in,
    sims_v,
    evo_out,
    evo_in,
    back_out,
    back_in,
    adj_v,
    sib_out,
    sib_in,
    term_v,
    hop_out,
    hop_in,
    lsem,
    ssem,
    rsem,
    bssem,
    brsem,
):
    tm = lax.axis_index("tm")
    sp = lax.axis_index("space")
    z, y = lax.div(tm, NX), lax.rem(tm, NX)
    x, core = lax.div(sp, 2), lax.rem(sp, 2)
    other = 1 - core

    def at_x(rel, c):
        return lax.rem(x + rel, NX) * 2 + (other if c else core)

    def plus(e):
        dz, dy = divmod(e, NX)
        return lax.rem(z + dz, NX) * NX + lax.rem(y + dy, NX)

    def minus(e):
        dz, dy = divmod(e, NX)
        return lax.rem(z + NX - dz, NX) * NX + lax.rem(y + NX - dy, NX)

    loads = []

    def load(src, dst):
        copy = pltpu.make_async_copy(src, dst, lsem.at[len(loads)])
        copy.start()
        loads.append(copy)
        return copy

    sends = []

    def send(src, dst, **where):
        n = len(sends)
        copy = pltpu.make_async_remote_copy(
            src_ref=src,
            dst_ref=dst,
            send_sem=ssem.at[n],
            recv_sem=rsem.at[n],
            device_id=where,
            device_id_type=MESH,
        )
        copy.start()
        sends.append(copy)
        return copy

    right, left = at_x(RIGHT, 0), at_x(LEFT, 0)
    sibling = at_x(OWN, 1)

    ld_state = load(state_hbm, state_v)
    ld_when = load(when_hbm, when_v)
    ld_block = load(block_hbm, block_v)
    ld_count = load(count_hbm, count_v)
    barrier = pltpu.get_barrier_semaphore()
    for d in (sibling, right, left):
        pl.semaphore_signal(barrier, inc=1, device_id={"space": d}, device_id_type=MESH)
    for e in (2, 1, 3, 2 * NX, NX, 3 * NX):
        pl.semaphore_signal(barrier, inc=1, device_id={"tm": plus(e)}, device_id_type=MESH)

    ld_state.wait()
    ld_space = {}

    def load_space(rel, c):
        cols = pl.ds(pl.multiple_of(at_x(rel, c) * COLS, COLS), COLS)
        ld_space[rel, c] = load(space_hbm.at[:, cols], space_v.at[rel, c])

    load_space(OWN, 0)
    load_space(OWN, 1)
    ld_time = load(time_hbm.at[:, pl.ds(pl.multiple_of(tm * ROWS, ROWS), ROWS)], time_v)
    for rel in (OPP, LEFT, RIGHT):
        load_space(rel, 0)
        load_space(rel, 1)
    ld_foot = load(foot_hbm, foot_v)
    ld_obs = load(obs_hbm, obs_v)
    ld_dep = load(dep_hbm, dep_v)
    ld_weight = load(weight_hbm, weight_v)

    for h in range(2):
        xall[OWN, 0, h] = state_v[:, h * HALF : (h + 1) * HALF].astype(BF16)
    ld_when.wait()
    ld_block.wait()
    ld_count.wait()
    lane = lax.broadcasted_iota(jnp.int32, (1, SLOTS), 1)
    code = when_v[...] * 8 + (block_v[...] - sp * NBLK)
    code = jnp.where(lane < count_v[...], code, -8)
    zero = jnp.zeros((1, SLOTS), jnp.int32)
    meta_out[0] = jnp.broadcast_to(jnp.concatenate([code, zero], axis=1), (8, 2 * SLOTS))
    meta_out[1] = jnp.broadcast_to(jnp.concatenate([zero, code], axis=1), (8, 2 * SLOTS))
    pl.semaphore_wait(barrier, 9)

    def block_to(rel, at, h, where):
        return send(xall.at[rel, 0, h], xall.at[at, 0, h], space=where)

    def block_over(rel, h):
        return send(xall.at[rel, 0, h], xall.at[rel, 1, h], space=sibling)

    got = {}
    got[LEFT, 0, 0] = block_to(OWN, LEFT, 0, right)
    got[RIGHT, 0, 1] = block_to(OWN, RIGHT, 1, left)
    odd = lax.rem(y, 2)
    from_y = [None] + [send(meta_out.at[odd], meta_y.at[y], tm=plus(d)) for d in range(1, NX)]
    meta_y[y] = meta_out[odd]
    got[LEFT, 0, 1] = block_to(OWN, LEFT, 1, right)
    got[RIGHT, 0, 0] = block_to(OWN, RIGHT, 0, left)
    for h in range(2):
        got[OWN, 1, h] = block_over(OWN, h)

    def add_spread(rel, c, h, first=False):
        term = nt_dot(xall[rel, c, h], space_v[rel, c, :, h * HALF : (h + 1) * HALF])
        if first:
            spread_v[...] = term
        else:
            spread_v[...] += term

    ld_space[OWN, 0].wait()
    add_spread(OWN, 0, 0, first=True)
    add_spread(OWN, 0, 1)
    for d in range(1, NX):
        from_y[d].wait_recv()
    line_out[0] = meta_y[0] + meta_y[1]
    line_out[1] = meta_y[2] + meta_y[3]
    from_z = [None] + [send(line_out, meta_z.at[z], tm=plus(d * NX)) for d in range(1, NX)]
    meta_z[z] = line_out[...]
    ld_space[OWN, 1].wait()
    for h in range(2):
        got[OWN, 1, h].wait_recv()
        add_spread(OWN, 1, h)
    ld_time.wait()
    time_t[...] = time_v[...].T.astype(BF16)
    for c in range(2):
        ld_space[OPP, c].wait()

        @pl.loop(0, COLS // BLK)
        def _(n, c=c):
            rows = pl.ds(pl.multiple_of(n * BLK, BLK), BLK)
            space_t[c, :, rows] = space_v[OPP, c, rows, :].T

    got[LEFT, 0, 0].wait_recv()
    got[OPP, 0, 0] = block_to(LEFT, OPP, 0, right)
    got[RIGHT, 0, 1].wait_recv()
    got[OPP, 0, 1] = block_to(RIGHT, OPP, 1, left)
    got[LEFT, 1, 0] = block_over(LEFT, 0)
    got[RIGHT, 1, 1] = block_over(RIGHT, 1)

    for rel, h in ((LEFT, 0), (RIGHT, 1)):
        ld_space[rel, 0].wait()
        add_spread(rel, 0, h)
    for rel, h in ((LEFT, 0), (RIGHT, 1)):
        ld_space[rel, 1].wait()
        got[rel, 1, h].wait_recv()
        add_spread(rel, 1, h)

    for d in range(1, NX):
        from_z[d].wait_recv()

    for d in range(NX):
        row = jnp.concatenate([meta_z[d, 0, 0:1, :], meta_z[d, 1, 0:1, :]], axis=1)
        when = lax.shift_right_arithmetic(row, 3)
        which = jnp.bitwise_and(row, 7)
        hot = lax.broadcasted_iota(jnp.int32, (TIMES, NX * SLOTS), 0) == when
        picked = nn_dot(time_t[...], jnp.where(hot, 1.0, 0.0).astype(BF16))
        slots = slice(d * NX * SLOTS, (d + 1) * NX * SLOTS)
        gt[:, slots] = picked.astype(BF16)
        picked_t = picked.T
        which_t = jnp.broadcast_to(which.astype(F32), (ROWS, NX * SLOTS)).T
        for b in range(NBLK):
            g4[slots, b * ROWS : (b + 1) * ROWS] = jnp.where(
                which_t == float(b), picked_t, 0.0
            ).astype(BF16)

    for rel, h in ((LEFT, 1), (RIGHT, 0)):
        got[rel, 0, h].wait_recv()
        got[rel, 1, h] = block_over(rel, h)
    for rel, h in ((LEFT, 1), (RIGHT, 0)):
        add_spread(rel, 0, h)
    for rel, h in ((LEFT, 1), (RIGHT, 0)):
        got[rel, 1, h].wait_recv()
        add_spread(rel, 1, h)
    for h in range(2):
        got[OPP, 0, h].wait_recv()
        got[OPP, 1, h] = block_over(OPP, h)
    for c in range(2):
        for h in range(2):
            if c:
                got[OPP, 1, h].wait_recv()
            spread_v[...] += nn_dot(xall[OPP, c, h], space_t[c, h * HALF : (h + 1) * HALF, :])

    spread4 = jnp.concatenate(
        [spread_v[:, b * BLK : (b + 1) * BLK].astype(BF16) for b in range(NBLK)], axis=0
    )
    from_part = [None] * NTM
    for dz in (2, 1, 3, 0):
        there = lax.rem(z + NX - dz, NX)
        rows = pl.ds(pl.multiple_of(there * NX * SLOTS, NX * SLOTS), NX * SLOTS)
        part = nn_dot(g4[rows, :], spread4)
        part_out[pl.ds(there * NX, NX)] = part.astype(BF16).reshape(NX, SLOTS, BLK)
        for dy in (2, 1, 3, 0):
            e = dz * NX + dy
            if e:
                from_part[e] = send(part_out.at[minus(e)], part_in.at[e], tm=minus(e))

    for b in range(NBLK):
        for d in range(NX):
            which = jnp.bitwise_and(
                jnp.concatenate([meta_z[d, 0, 0:1, :], meta_z[d, 1, 0:1, :]], axis=1), 7
            )
            slots = slice(d * NX * SLOTS, (d + 1) * NX * SLOTS)
            gt4[b * ROWS : (b + 1) * ROWS, slots] = jnp.where(
                which == b, gt[:, slots].astype(F32), 0.0
            ).astype(BF16)
    ld_foot.wait()

    @pl.loop(0, SLOTS // 4)
    def _(k):
        for i in range(4):
            foot_t[4 * k + i] = foot_v[4 * k + i].T

    ld_obs.wait()
    pick = jnp.where(
        lax.broadcasted_iota(jnp.int32, (SLOTS, SLOTS), 0) == obs_v[...] - tm * SLOTS, 1.0, 0.0
    )
    pick_low = pick.astype(BF16)
    pick_t = pick.T.astype(BF16)
    ld_dep.wait()
    ld_weight.wait()

    flux = part_out[tm].astype(F32)
    for e in FAR_FIRST[::-1]:
        from_part[e].wait_recv()
        flux += part_in[e].astype(F32)
    flux = flux.astype(BF16)

    group = 16
    row16 = lax.broadcasted_iota(jnp.int32, (group, BLK), 0)
    for g in range(SLOTS // group):
        mine = flux[g * group : (g + 1) * group, :]
        acc = jnp.zeros((group, OBS), F32)
        for k in range(group):
            acc += nn_dot(jnp.where(row16 == k, mine, jnp.zeros_like(mine)), foot_t[g * group + k])
        sims_v[g * group : (g + 1) * group, :] = acc
    sims = sims_v[...]
    sims_hi = sims.astype(BF16)
    sims_lo = (sims - sims_hi.astype(F32)).astype(BF16)
    evolved = nn_dot(pick_low, sims_hi) + nn_dot(pick_low, sims_lo)
    evo_out[...] = evolved.astype(BF16)
    from_evo = []
    for rel, c in ((OPP, 1), (OPP, 0), (RIGHT, 1), (LEFT, 1), (RIGHT, 0), (LEFT, 0), (OWN, 1)):
        from_evo.append(send(evo_out, evo_in.at[len(from_evo)], space=at_x(rel, c)))
    for n in range(NSP - 1)[::-1]:
        from_evo[n].wait_recv()
        evolved += evo_in[n].astype(F32)
    depart = (weight_v[...] * (evolved - dep_v[...])).astype(BF16)
    mine_dep = nn_dot(pick_t, depart).astype(BF16)

    row16 = lax.broadcasted_iota(jnp.int32, (group, OBS), 0)
    for g in range(SLOTS // group):
        mine = mine_dep[g * group : (g + 1) * group, :]
        acc = jnp.zeros((group, BLK), F32)
        for k in range(group):
            acc += nn_dot(jnp.where(row16 == k, mine, jnp.zeros_like(mine)), foot_v[g * group + k])
        back_out[g * group : (g + 1) * group, :] = acc.astype(BF16)
    def back_copy(dest, source):
        return pltpu.make_async_remote_copy(
            src_ref=back_out,
            dst_ref=back_in.at[source],
            send_sem=bssem.at[dest],
            recv_sem=brsem.at[source],
            device_id={"tm": dest},
            device_id_type=MESH,
        )

    for d in range(NTM):

        @pl.when(tm != d)
        def _(d=d):
            back_copy(d, tm).start()

    back_in[tm] = back_out[...]

    adj = jnp.zeros((NBLK * ROWS, BLK), F32)
    for q in range(4):
        for e in range(4 * q, 4 * q + 4):

            @pl.when(tm != e)
            def _(e=e):
                back_copy(e, e).wait_recv()

        adj += nn_dot(
            gt4[:, q * 4 * SLOTS : (q + 1) * 4 * SLOTS],
            back_in[4 * q : 4 * q + 4].reshape(4 * SLOTS, BLK),
        )
    for b in range(NBLK):
        adj_v[:, b * BLK : (b + 1) * BLK] = adj[b * ROWS : (b + 1) * ROWS, :].astype(BF16)

    def terms(rel, c, h):
        return nn_dot(adj_v[...], space_v[rel, c, :, h * HALF : (h + 1) * HALF])

    from_pair = {}

    def to_sibling(rel, h):
        sib_out[rel, h] = terms(rel, 1, h).astype(BF16)
        from_pair[rel, h] = send(sib_out.at[rel, h], sib_in.at[rel, h], space=sibling)

    def own_terms(rel, h):
        term_v[rel, h] = terms(rel, 0, h)

    def pair(rel, h):
        from_pair[rel, h].wait_recv()
        return term_v[rel, h] + sib_in[rel, h].astype(F32)

    def hop(n, value, where):
        hop_out[n] = value.astype(BF16)
        return send(hop_out.at[n], hop_in.at[n], space=where)

    to_sibling(OPP, 0)
    to_sibling(OPP, 1)
    own_terms(OPP, 0)
    own_terms(OPP, 1)
    to_sibling(LEFT, 0)
    to_sibling(RIGHT, 1)
    far_left = hop(0, pair(OPP, 0), right)
    far_right = hop(1, pair(OPP, 1), left)
    own_terms(LEFT, 0)
    own_terms(RIGHT, 1)
    near_right = hop(2, pair(LEFT, 0), left)
    near_left = hop(3, pair(RIGHT, 1), right)
    to_sibling(RIGHT, 0)
    to_sibling(LEFT, 1)
    own_terms(RIGHT, 0)
    own_terms(LEFT, 1)
    term_v[RIGHT, 0] = pair(RIGHT, 0)
    term_v[LEFT, 1] = pair(LEFT, 1)
    far_left.wait_recv()
    last_left = hop(4, term_v[RIGHT, 0] + hop_in[0].astype(F32), right)
    far_right.wait_recv()
    last_right = hop(5, term_v[LEFT, 1] + hop_in[1].astype(F32), left)
    to_sibling(OWN, 0)
    to_sibling(OWN, 1)
    own_terms(OWN, 0)
    own_terms(OWN, 1)
    for h in range(2):
        cols = slice(h * HALF, (h + 1) * HALF)
        out_v[:, cols] = state_v[:, cols] + pair(OWN, h)
    near_right.wait_recv()
    out_v[:, :HALF] += hop_in[2].astype(F32)
    near_left.wait_recv()
    out_v[:, HALF:] += hop_in[3].astype(F32)
    for h, copy in enumerate((last_left, last_right)):
        cols = slice(h * HALF, (h + 1) * HALF)
        copy.wait_recv()
        out_v[:, cols] += hop_in[4 + h].astype(F32)
    for copy in sends:
        copy.wait_send()
    for d in range(NTM):

        @pl.when(tm != d)
        def _(d=d):
            back_copy(d, tm).wait_send()


N_LOADS = 17
N_SENDS = 3 + 3 + 6 + 8 + 15 + 7 + 8 + 6


def local(
    state,
    space_factor,
    time_factor,
    footprints,
    tile_obs,
    tile_block,
    tile_time,
    tile_count,
    obs_dep,
    obs_weight,
):
    any_spec = pl.BlockSpec(memory_space=pl.ANY)
    vm = pltpu.VMEM
    i32 = jnp.int32
    return pl.pallas_call(
        kernel,
        out_shape=pltpu.VMEM((ROWS, COLS), F32),
        in_specs=[any_spec] * 10,
        out_specs=pl.BlockSpec(memory_space=pltpu.VMEM),
        scratch_shapes=[
            vm((ROWS, COLS), F32),
            vm((NX, 2, COLS, COLS), BF16),
            vm((2, COLS, COLS), BF16),
            vm((TIMES, ROWS), F32),
            vm((SLOTS, OBS, BLK), BF16),
            vm((SLOTS, BLK, OBS), BF16),
            vm((1, SLOTS), i32),
            vm((1, SLOTS), i32),
            vm((1, SLOTS), i32),
            vm((1, 1), i32),
            vm((SLOTS, OBS), F32),
            vm((SLOTS, OBS), F32),
            vm((NX, 2, 2, ROWS, HALF), BF16),
            vm((ROWS, COLS), F32),
            vm((ROWS, TIMES), BF16),
            vm((2, 8, 2 * SLOTS), i32),
            vm((NX, 8, 2 * SLOTS), i32),
            vm((2, 8, 2 * SLOTS), i32),
            vm((NX, 2, 8, 2 * SLOTS), i32),
            vm((ROWS, NTM * SLOTS), BF16),
            vm((NBLK * ROWS, NTM * SLOTS), BF16),
            vm((NTM * SLOTS, NBLK * ROWS), BF16),
            vm((NTM, SLOTS, BLK), BF16),
            vm((NTM, SLOTS, BLK), BF16),
            vm((SLOTS, OBS), F32),
            vm((SLOTS, OBS), BF16),
            vm((NSP - 1, SLOTS, OBS), BF16),
            vm((SLOTS, BLK), BF16),
            vm((NTM, SLOTS, BLK), BF16),
            vm((ROWS, COLS), BF16),
            vm((NX, 2, ROWS, HALF), BF16),
            vm((NX, 2, ROWS, HALF), BF16),
            vm((NX, 2, ROWS, HALF), F32),
            vm((6, ROWS, HALF), BF16),
            vm((6, ROWS, HALF), BF16),
            pltpu.SemaphoreType.DMA((N_LOADS,)),
            pltpu.SemaphoreType.DMA((N_SENDS,)),
            pltpu.SemaphoreType.DMA((N_SENDS,)),
            pltpu.SemaphoreType.DMA((NTM,)),
            pltpu.SemaphoreType.DMA((NTM,)),
        ],
        compiler_params=pltpu.CompilerParams(
            collective_id=0, has_side_effects=True, vmem_limit_bytes=56 * 1024 * 1024
        ),
    )(
        state,
        space_factor,
        time_factor,
        footprints.reshape(SLOTS, OBS, BLK),
        tile_obs.reshape(1, SLOTS),
        tile_block.reshape(1, SLOTS),
        tile_time.reshape(1, SLOTS),
        tile_count,
        obs_dep,
        obs_weight,
    )


def solution(mesh):
    return jax.shard_map(
        local,
        mesh=mesh,
        in_specs=(
            P("tm", "space"),
            P("space", None),
            P(),
            P("tm", "space", None, None),
            P("tm", "space"),
            P("tm", "space"),
            P("tm", "space"),
            P("tm", "space"),
            P("tm", None),
            P("tm", None),
        ),
        out_specs=P("tm", "space"),
        check_vma=False,
    )
```

```python
import functools

import jax
import jax.numpy as jnp
from jax import lax
from jax.experimental import pallas as pl
from jax.experimental.pallas import tpu as pltpu
from jax.sharding import PartitionSpec as P

MESH = pl.DeviceIdType.MESH
F32 = jnp.float32
BF16 = jnp.bfloat16
NX = 4
NTM = 16
NSP = 8
SLOTS = 64
ROWS = 128
COLS = 1024
HALF = COLS // 2
BLK = 256
NBLK = COLS // BLK
OBS = 128
TIMES = 2048
OWN, RIGHT, OPP, LEFT = 0, 1, 2, 3


FAR_FIRST = (10, 11, 6, 9, 14, 2, 8, 7, 5, 13, 15, 3, 1, 12, 4)


def nt_dot(a, b):
    return lax.dot_general(a, b, (((1,), (1,)), ((), ())), preferred_element_type=F32)


def nn_dot(a, b):
    return jnp.dot(a, b, preferred_element_type=F32)


def kernel(
    state_hbm,
    space_hbm,
    time_hbm,
    foot_hbm,
    obs_hbm,
    block_hbm,
    when_hbm,
    count_hbm,
    dep_hbm,
    weight_hbm,
    out_v,
    state_v,
    space_v,
    space_t,
    time_v,
    foot_v,
    foot_t,
    obs_v,
    block_v,
    when_v,
    count_v,
    dep_v,
    weight_v,
    xall,
    spread_v,
    time_t,
    meta_out,
    meta_y,
    line_out,
    meta_z,
    gt,
    gt4,
    g4,
    part_out,
    part_in,
    sims_v,
    evo_out,
    evo_in,
    back_out,
    back_in,
    adj_v,
    sib_out,
    sib_in,
    term_v,
    hop_out,
    hop_in,
    lsem,
    ssem,
    rsem,
    bssem,
    brsem,
):
    tm = lax.axis_index("tm")
    sp = lax.axis_index("space")
    z, y = lax.div(tm, NX), lax.rem(tm, NX)
    x, core = lax.div(sp, 2), lax.rem(sp, 2)
    other = 1 - core

    def at_x(rel, c):
        return lax.rem(x + rel, NX) * 2 + (other if c else core)

    def plus(e):
        dz, dy = divmod(e, NX)
        return lax.rem(z + dz, NX) * NX + lax.rem(y + dy, NX)

    def minus(e):
        dz, dy = divmod(e, NX)
        return lax.rem(z + NX - dz, NX) * NX + lax.rem(y + NX - dy, NX)

    loads = []

    def load(src, dst):
        copy = pltpu.make_async_copy(src, dst, lsem.at[len(loads)])
        copy.start()
        loads.append(copy)
        return copy

    sends = []

    def send(src, dst, **where):
        n = len(sends)
        copy = pltpu.make_async_remote_copy(
            src_ref=src,
            dst_ref=dst,
            send_sem=ssem.at[n],
            recv_sem=rsem.at[n],
            device_id=where,
            device_id_type=MESH,
        )
        copy.start()
        sends.append(copy)
        return copy

    right, left = at_x(RIGHT, 0), at_x(LEFT, 0)
    sibling = at_x(OWN, 1)

    ld_state = load(state_hbm, state_v)
    ld_when = load(when_hbm, when_v)
    ld_block = load(block_hbm, block_v)
    ld_count = load(count_hbm, count_v)
    barrier = pltpu.get_barrier_semaphore()
    for d in (sibling, right, left):
        pl.semaphore_signal(barrier, inc=1, device_id={"space": d}, device_id_type=MESH)
    for e in (2, 1, 3, 2 * NX, NX, 3 * NX):
        pl.semaphore_signal(barrier, inc=1, device_id={"tm": plus(e)}, device_id_type=MESH)

    ld_state.wait()
    ld_space = {}

    def load_space(rel, c):
        cols = pl.ds(pl.multiple_of(at_x(rel, c) * COLS, COLS), COLS)
        ld_space[rel, c] = load(space_hbm.at[:, cols], space_v.at[rel, c])

    load_space(OWN, 0)
    load_space(OWN, 1)
    ld_time = load(time_hbm.at[:, pl.ds(pl.multiple_of(tm * ROWS, ROWS), ROWS)], time_v)
    for rel in (OPP, LEFT, RIGHT):
        load_space(rel, 0)
        load_space(rel, 1)
    ld_foot = load(foot_hbm, foot_v)
    ld_obs = load(obs_hbm, obs_v)
    ld_dep = load(dep_hbm, dep_v)
    ld_weight = load(weight_hbm, weight_v)

    for h in range(2):
        xall[OWN, 0, h] = state_v[:, h * HALF : (h + 1) * HALF].astype(BF16)
    ld_when.wait()
    ld_block.wait()
    ld_count.wait()
    lane = lax.broadcasted_iota(jnp.int32, (1, SLOTS), 1)
    code = when_v[...] * 8 + (block_v[...] - sp * NBLK)
    code = jnp.where(lane < count_v[...], code, -8)
    zero = jnp.zeros((1, SLOTS), jnp.int32)
    meta_out[0] = jnp.broadcast_to(jnp.concatenate([code, zero], axis=1), (8, 2 * SLOTS))
    meta_out[1] = jnp.broadcast_to(jnp.concatenate([zero, code], axis=1), (8, 2 * SLOTS))
    pl.semaphore_wait(barrier, 9)

    def block_to(rel, at, h, where):
        return send(xall.at[rel, 0, h], xall.at[at, 0, h], space=where)

    def block_over(rel, h):
        return send(xall.at[rel, 0, h], xall.at[rel, 1, h], space=sibling)

    got = {}
    got[LEFT, 0, 0] = block_to(OWN, LEFT, 0, right)
    got[RIGHT, 0, 1] = block_to(OWN, RIGHT, 1, left)
    odd = lax.rem(y, 2)
    from_y = [None] + [send(meta_out.at[odd], meta_y.at[y], tm=plus(d)) for d in range(1, NX)]
    meta_y[y] = meta_out[odd]
    got[LEFT, 0, 1] = block_to(OWN, LEFT, 1, right)
    got[RIGHT, 0, 0] = block_to(OWN, RIGHT, 0, left)
    for h in range(2):
        got[OWN, 1, h] = block_over(OWN, h)

    def add_spread(rel, c, h, first=False):
        term = nt_dot(xall[rel, c, h], space_v[rel, c, :, h * HALF : (h + 1) * HALF])
        if first:
            spread_v[...] = term
        else:
            spread_v[...] += term

    ld_space[OWN, 0].wait()
    add_spread(OWN, 0, 0, first=True)
    add_spread(OWN, 0, 1)
    for d in range(1, NX):
        from_y[d].wait_recv()
    line_out[0] = meta_y[0] + meta_y[1]
    line_out[1] = meta_y[2] + meta_y[3]
    from_z = [None] + [send(line_out, meta_z.at[z], tm=plus(d * NX)) for d in range(1, NX)]
    meta_z[z] = line_out[...]
    ld_space[OWN, 1].wait()
    for h in range(2):
        got[OWN, 1, h].wait_recv()
        add_spread(OWN, 1, h)
    ld_time.wait()
    time_t[...] = time_v[...].T.astype(BF16)
    for c in range(2):
        ld_space[OPP, c].wait()

        @pl.loop(0, COLS // BLK)
        def _(n, c=c):
            rows = pl.ds(pl.multiple_of(n * BLK, BLK), BLK)
            space_t[c, :, rows] = space_v[OPP, c, rows, :].T

    got[LEFT, 0, 0].wait_recv()
    got[OPP, 0, 0] = block_to(LEFT, OPP, 0, right)
    got[RIGHT, 0, 1].wait_recv()
    got[OPP, 0, 1] = block_to(RIGHT, OPP, 1, left)
    got[LEFT, 1, 0] = block_over(LEFT, 0)
    got[RIGHT, 1, 1] = block_over(RIGHT, 1)

    for rel, h in ((LEFT, 0), (RIGHT, 1)):
        ld_space[rel, 0].wait()
        add_spread(rel, 0, h)
    for rel, h in ((LEFT, 0), (RIGHT, 1)):
        ld_space[rel, 1].wait()
        got[rel, 1, h].wait_recv()
        add_spread(rel, 1, h)

    for d in range(1, NX):
        from_z[d].wait_recv()

    for d in range(NX):
        row = jnp.concatenate([meta_z[d, 0, 0:1, :], meta_z[d, 1, 0:1, :]], axis=1)
        when = lax.shift_right_arithmetic(row, 3)
        which = jnp.bitwise_and(row, 7)
        hot = lax.broadcasted_iota(jnp.int32, (TIMES, NX * SLOTS), 0) == when
        picked = nn_dot(time_t[...], jnp.where(hot, 1.0, 0.0).astype(BF16))
        slots = slice(d * NX * SLOTS, (d + 1) * NX * SLOTS)
        gt[:, slots] = picked.astype(BF16)
        picked_t = picked.T
        which_t = jnp.broadcast_to(which.astype(F32), (ROWS, NX * SLOTS)).T
        for b in range(NBLK):
            g4[slots, b * ROWS : (b + 1) * ROWS] = jnp.where(
                which_t == float(b), picked_t, 0.0
            ).astype(BF16)

    for rel, h in ((LEFT, 1), (RIGHT, 0)):
        got[rel, 0, h].wait_recv()
        got[rel, 1, h] = block_over(rel, h)
    for rel, h in ((LEFT, 1), (RIGHT, 0)):
        add_spread(rel, 0, h)
    for rel, h in ((LEFT, 1), (RIGHT, 0)):
        got[rel, 1, h].wait_recv()
        add_spread(rel, 1, h)
    for h in range(2):
        got[OPP, 0, h].wait_recv()
        got[OPP, 1, h] = block_over(OPP, h)
    for c in range(2):
        for h in range(2):
            if c:
                got[OPP, 1, h].wait_recv()
            spread_v[...] += nn_dot(xall[OPP, c, h], space_t[c, h * HALF : (h + 1) * HALF, :])

    spread4 = jnp.concatenate(
        [spread_v[:, b * BLK : (b + 1) * BLK].astype(BF16) for b in range(NBLK)], axis=0
    )
    from_part = [None] * NTM
    for dz in (2, 1, 3, 0):
        there = lax.rem(z + NX - dz, NX)
        rows = pl.ds(pl.multiple_of(there * NX * SLOTS, NX * SLOTS), NX * SLOTS)
        part = nn_dot(g4[rows, :], spread4)
        part_out[pl.ds(there * NX, NX)] = part.astype(BF16).reshape(NX, SLOTS, BLK)
        for dy in (2, 1, 3, 0):
            e = dz * NX + dy
            if e:
                from_part[e] = send(part_out.at[minus(e)], part_in.at[e], tm=minus(e))

    for b in range(NBLK):
        for d in range(NX):
            which = jnp.bitwise_and(
                jnp.concatenate([meta_z[d, 0, 0:1, :], meta_z[d, 1, 0:1, :]], axis=1), 7
            )
            slots = slice(d * NX * SLOTS, (d + 1) * NX * SLOTS)
            gt4[b * ROWS : (b + 1) * ROWS, slots] = jnp.where(
                which == b, gt[:, slots].astype(F32), 0.0
            ).astype(BF16)
    ld_foot.wait()

    @pl.loop(0, SLOTS // 4)
    def _(k):
        for i in range(4):
            foot_t[4 * k + i] = foot_v[4 * k + i].T

    ld_obs.wait()
    pick = jnp.where(
        lax.broadcasted_iota(jnp.int32, (SLOTS, SLOTS), 0) == obs_v[...] - tm * SLOTS, 1.0, 0.0
    )
    pick_low = pick.astype(BF16)
    pick_t = pick.T.astype(BF16)
    ld_dep.wait()
    ld_weight.wait()

    flux = part_out[tm].astype(F32)
    for e in FAR_FIRST[::-1]:
        from_part[e].wait_recv()
        flux += part_in[e].astype(F32)
    flux = flux.astype(BF16)

    group = 16
    row16 = lax.broadcasted_iota(jnp.int32, (group, BLK), 0)
    for g in range(SLOTS // group):
        mine = flux[g * group : (g + 1) * group, :]
        acc = jnp.zeros((group, OBS), F32)
        for k in range(group):
            acc += nn_dot(jnp.where(row16 == k, mine, jnp.zeros_like(mine)), foot_t[g * group + k])
        sims_v[g * group : (g + 1) * group, :] = acc
    sims = sims_v[...]
    sims_hi = sims.astype(BF16)
    sims_lo = (sims - sims_hi.astype(F32)).astype(BF16)
    evolved = nn_dot(pick_low, sims_hi) + nn_dot(pick_low, sims_lo)
    evo_out[...] = evolved.astype(BF16)
    from_evo = []
    for rel, c in ((OPP, 1), (OPP, 0), (RIGHT, 1), (LEFT, 1), (RIGHT, 0), (LEFT, 0), (OWN, 1)):
        from_evo.append(send(evo_out, evo_in.at[len(from_evo)], space=at_x(rel, c)))
    for n in range(NSP - 1)[::-1]:
        from_evo[n].wait_recv()
        evolved += evo_in[n].astype(F32)
    depart = (weight_v[...] * (evolved - dep_v[...])).astype(BF16)
    mine_dep = nn_dot(pick_t, depart).astype(BF16)

    row16 = lax.broadcasted_iota(jnp.int32, (group, OBS), 0)
    for g in range(SLOTS // group):
        mine = mine_dep[g * group : (g + 1) * group, :]
        acc = jnp.zeros((group, BLK), F32)
        for k in range(group):
            acc += nn_dot(jnp.where(row16 == k, mine, jnp.zeros_like(mine)), foot_v[g * group + k])
        back_out[g * group : (g + 1) * group, :] = acc.astype(BF16)
    def back_copy(dest, source):
        return pltpu.make_async_remote_copy(
            src_ref=back_out,
            dst_ref=back_in.at[source],
            send_sem=bssem.at[dest],
            recv_sem=brsem.at[source],
            device_id={"tm": dest},
            device_id_type=MESH,
        )

    for d in range(NTM):

        @pl.when(tm != d)
        def _(d=d):
            back_copy(d, tm).start()

    back_in[tm] = back_out[...]
    left_here = len(sends)
    for copy in sends:
        copy.wait_send()

    adj = jnp.zeros((NBLK * ROWS, BLK), F32)
    for q in range(4):
        for e in range(4 * q, 4 * q + 4):

            @pl.when(tm != e)
            def _(e=e):
                back_copy(e, e).wait_recv()

        adj += nn_dot(
            gt4[:, q * 4 * SLOTS : (q + 1) * 4 * SLOTS],
            back_in[4 * q : 4 * q + 4].reshape(4 * SLOTS, BLK),
        )
    for b in range(NBLK):
        adj_v[:, b * BLK : (b + 1) * BLK] = adj[b * ROWS : (b + 1) * ROWS, :].astype(BF16)

    def terms(rel, c, h):
        return nn_dot(adj_v[...], space_v[rel, c, :, h * HALF : (h + 1) * HALF])

    from_pair = {}

    def to_sibling(rel, h):
        sib_out[rel, h] = terms(rel, 1, h).astype(BF16)
        from_pair[rel, h] = send(sib_out.at[rel, h], sib_in.at[rel, h], space=sibling)

    def own_terms(rel, h):
        term_v[rel, h] = terms(rel, 0, h)

    def pair(rel, h):
        from_pair[rel, h].wait_recv()
        return term_v[rel, h] + sib_in[rel, h].astype(F32)

    def hop(n, value, where):
        hop_out[n] = value.astype(BF16)
        return send(hop_out.at[n], hop_in.at[n], space=where)

    to_sibling(OPP, 0)
    to_sibling(OPP, 1)
    own_terms(OPP, 0)
    own_terms(OPP, 1)
    to_sibling(LEFT, 0)
    to_sibling(RIGHT, 1)
    far_left = hop(0, pair(OPP, 0), right)
    far_right = hop(1, pair(OPP, 1), left)
    own_terms(LEFT, 0)
    own_terms(RIGHT, 1)
    near_right = hop(2, pair(LEFT, 0), left)
    near_left = hop(3, pair(RIGHT, 1), right)
    to_sibling(RIGHT, 0)
    to_sibling(LEFT, 1)
    own_terms(RIGHT, 0)
    own_terms(LEFT, 1)
    term_v[RIGHT, 0] = pair(RIGHT, 0)
    term_v[LEFT, 1] = pair(LEFT, 1)
    to_sibling(OWN, 0)
    to_sibling(OWN, 1)
    for d in range(NTM):

        @pl.when(tm != d)
        def _(d=d):
            back_copy(d, tm).wait_send()

    far_left.wait_recv()
    last_left = hop(4, term_v[RIGHT, 0] + hop_in[0].astype(F32), right)
    far_right.wait_recv()
    last_right = hop(5, term_v[LEFT, 1] + hop_in[1].astype(F32), left)
    own_terms(OWN, 0)
    own_terms(OWN, 1)
    for h in range(2):
        cols = slice(h * HALF, (h + 1) * HALF)
        out_v[:, cols] = state_v[:, cols] + pair(OWN, h)
    for copy in sends[left_here:-2]:
        copy.wait_send()
    near_right.wait_recv()
    out_v[:, :HALF] += hop_in[2].astype(F32)
    near_left.wait_recv()
    out_v[:, HALF:] += hop_in[3].astype(F32)
    for h, copy in enumerate((last_left, last_right)):
        cols = slice(h * HALF, (h + 1) * HALF)
        copy.wait_recv()
        out_v[:, cols] += hop_in[4 + h].astype(F32)
    for copy in sends[-2:]:
        copy.wait_send()


N_LOADS = 17
N_SENDS = 3 + 3 + 6 + 8 + 15 + 7 + 8 + 6


def local(
    state,
    space_factor,
    time_factor,
    footprints,
    tile_obs,
    tile_block,
    tile_time,
    tile_count,
    obs_dep,
    obs_weight,
):
    any_spec = pl.BlockSpec(memory_space=pl.ANY)
    vm = pltpu.VMEM
    i32 = jnp.int32
    return pl.pallas_call(
        kernel,
        out_shape=pltpu.VMEM((ROWS, COLS), F32),
        in_specs=[any_spec] * 10,
        out_specs=pl.BlockSpec(memory_space=pltpu.VMEM),
        scratch_shapes=[
            vm((ROWS, COLS), F32),
            vm((NX, 2, COLS, COLS), BF16),
            vm((2, COLS, COLS), BF16),
            vm((TIMES, ROWS), F32),
            vm((SLOTS, OBS, BLK), BF16),
            vm((SLOTS, BLK, OBS), BF16),
            vm((1, SLOTS), i32),
            vm((1, SLOTS), i32),
            vm((1, SLOTS), i32),
            vm((1, 1), i32),
            vm((SLOTS, OBS), F32),
            vm((SLOTS, OBS), F32),
            vm((NX, 2, 2, ROWS, HALF), BF16),
            vm((ROWS, COLS), F32),
            vm((ROWS, TIMES), BF16),
            vm((2, 8, 2 * SLOTS), i32),
            vm((NX, 8, 2 * SLOTS), i32),
            vm((2, 8, 2 * SLOTS), i32),
            vm((NX, 2, 8, 2 * SLOTS), i32),
            vm((ROWS, NTM * SLOTS), BF16),
            vm((NBLK * ROWS, NTM * SLOTS), BF16),
            vm((NTM * SLOTS, NBLK * ROWS), BF16),
            vm((NTM, SLOTS, BLK), BF16),
            vm((NTM, SLOTS, BLK), BF16),
            vm((SLOTS, OBS), F32),
            vm((SLOTS, OBS), BF16),
            vm((NSP - 1, SLOTS, OBS), BF16),
            vm((SLOTS, BLK), BF16),
            vm((NTM, SLOTS, BLK), BF16),
            vm((ROWS, COLS), BF16),
            vm((NX, 2, ROWS, HALF), BF16),
            vm((NX, 2, ROWS, HALF), BF16),
            vm((NX, 2, ROWS, HALF), F32),
            vm((6, ROWS, HALF), BF16),
            vm((6, ROWS, HALF), BF16),
            pltpu.SemaphoreType.DMA((N_LOADS,)),
            pltpu.SemaphoreType.DMA((N_SENDS,)),
            pltpu.SemaphoreType.DMA((N_SENDS,)),
            pltpu.SemaphoreType.DMA((NTM,)),
            pltpu.SemaphoreType.DMA((NTM,)),
        ],
        compiler_params=pltpu.CompilerParams(
            collective_id=0, has_side_effects=True, vmem_limit_bytes=56 * 1024 * 1024
        ),
    )(
        state,
        space_factor,
        time_factor,
        footprints.reshape(SLOTS, OBS, BLK),
        tile_obs.reshape(1, SLOTS),
        tile_block.reshape(1, SLOTS),
        tile_time.reshape(1, SLOTS),
        tile_count,
        obs_dep,
        obs_weight,
    )


def solution(mesh):
    return jax.shard_map(
        local,
        mesh=mesh,
        in_specs=(
            P("tm", "space"),
            P("space", None),
            P(),
            P("tm", "space", None, None),
            P("tm", "space"),
            P("tm", "space"),
            P("tm", "space"),
            P("tm", "space"),
            P("tm", None),
            P("tm", None),
        ),
        out_specs=P("tm", "space"),
        check_vma=False,
    )
```

```python
import functools

import jax
import jax.numpy as jnp
from jax import lax
from jax.experimental import pallas as pl
from jax.experimental.pallas import tpu as pltpu
from jax.sharding import PartitionSpec as P

MESH = pl.DeviceIdType.MESH
F32 = jnp.float32
BF16 = jnp.bfloat16
NX = 4
NTM = 16
NSP = 8
SLOTS = 64
ROWS = 128
COLS = 1024
HALF = COLS // 2
BLK = 256
NBLK = COLS // BLK
OBS = 128
TIMES = 2048
OWN, RIGHT, OPP, LEFT = 0, 1, 2, 3


FAR_FIRST = (10, 11, 6, 9, 14, 2, 8, 7, 5, 13, 15, 3, 1, 12, 4)


def nt_dot(a, b):
    return lax.dot_general(a, b, (((1,), (1,)), ((), ())), preferred_element_type=F32)


def nn_dot(a, b):
    return jnp.dot(a, b, preferred_element_type=F32)


def kernel(
    state_hbm,
    space_hbm,
    time_hbm,
    foot_hbm,
    obs_hbm,
    block_hbm,
    when_hbm,
    count_hbm,
    dep_hbm,
    weight_hbm,
    out_v,
    state_v,
    space_v,
    space_t,
    time_v,
    foot_v,
    foot_t,
    obs_v,
    block_v,
    when_v,
    count_v,
    dep_v,
    weight_v,
    xall,
    spread_v,
    time_t,
    meta_out,
    meta_y,
    line_out,
    meta_z,
    gt,
    gt4,
    g4,
    part_out,
    part_in,
    sims_v,
    evo_out,
    evo_in,
    back_out,
    back_in,
    adj_v,
    sib_out,
    sib_in,
    term_v,
    hop_out,
    hop_in,
    lsem,
    ssem,
    rsem,
    bssem,
    brsem,
):
    tm = lax.axis_index("tm")
    sp = lax.axis_index("space")
    z, y = lax.div(tm, NX), lax.rem(tm, NX)
    x, core = lax.div(sp, 2), lax.rem(sp, 2)
    other = 1 - core

    def at_x(rel, c):
        return lax.rem(x + rel, NX) * 2 + (other if c else core)

    def plus(e):
        dz, dy = divmod(e, NX)
        return lax.rem(z + dz, NX) * NX + lax.rem(y + dy, NX)

    def minus(e):
        dz, dy = divmod(e, NX)
        return lax.rem(z + NX - dz, NX) * NX + lax.rem(y + NX - dy, NX)

    loads = []

    def load(src, dst):
        copy = pltpu.make_async_copy(src, dst, lsem.at[len(loads)])
        copy.start()
        loads.append(copy)
        return copy

    sends = []

    def send(src, dst, **where):
        n = len(sends)
        copy = pltpu.make_async_remote_copy(
            src_ref=src,
            dst_ref=dst,
            send_sem=ssem.at[n],
            recv_sem=rsem.at[n],
            device_id=where,
            device_id_type=MESH,
        )
        copy.start()
        sends.append(copy)
        return copy

    right, left = at_x(RIGHT, 0), at_x(LEFT, 0)
    sibling = at_x(OWN, 1)

    ld_state = load(state_hbm, state_v)
    ld_when = load(when_hbm, when_v)
    ld_block = load(block_hbm, block_v)
    ld_count = load(count_hbm, count_v)
    barrier = pltpu.get_barrier_semaphore()
    for d in (sibling, right, left):
        pl.semaphore_signal(barrier, inc=1, device_id={"space": d}, device_id_type=MESH)
    for e in (2, 1, 3, 2 * NX, NX, 3 * NX):
        pl.semaphore_signal(barrier, inc=1, device_id={"tm": plus(e)}, device_id_type=MESH)

    ld_state.wait()
    ld_space = {}

    def load_space(rel, c):
        cols = pl.ds(pl.multiple_of(at_x(rel, c) * COLS, COLS), COLS)
        ld_space[rel, c] = load(space_hbm.at[:, cols], space_v.at[rel, c])

    load_space(OWN, 0)
    load_space(OWN, 1)
    ld_time = load(time_hbm.at[:, pl.ds(pl.multiple_of(tm * ROWS, ROWS), ROWS)], time_v)
    for rel in (OPP, LEFT, RIGHT):
        load_space(rel, 0)
        load_space(rel, 1)
    ld_foot = load(foot_hbm, foot_v)
    ld_obs = load(obs_hbm, obs_v)
    ld_dep = load(dep_hbm, dep_v)
    ld_weight = load(weight_hbm, weight_v)

    for h in range(2):
        xall[OWN, 0, h] = state_v[:, h * HALF : (h + 1) * HALF].astype(BF16)
    ld_when.wait()
    ld_block.wait()
    ld_count.wait()
    lane = lax.broadcasted_iota(jnp.int32, (1, SLOTS), 1)
    code = when_v[...] * 8 + (block_v[...] - sp * NBLK)
    code = jnp.where(lane < count_v[...], code, -8)
    zero = jnp.zeros((1, SLOTS), jnp.int32)
    meta_out[0] = jnp.broadcast_to(jnp.concatenate([code, zero], axis=1), (8, 2 * SLOTS))
    meta_out[1] = jnp.broadcast_to(jnp.concatenate([zero, code], axis=1), (8, 2 * SLOTS))
    pl.semaphore_wait(barrier, 9)

    def block_to(rel, at, h, where):
        return send(xall.at[rel, 0, h], xall.at[at, 0, h], space=where)

    def block_over(rel, h):
        return send(xall.at[rel, 0, h], xall.at[rel, 1, h], space=sibling)

    got = {}
    got[LEFT, 0, 0] = block_to(OWN, LEFT, 0, right)
    got[RIGHT, 0, 1] = block_to(OWN, RIGHT, 1, left)
    odd = lax.rem(y, 2)
    from_y = [None] + [send(meta_out.at[odd], meta_y.at[y], tm=plus(d)) for d in range(1, NX)]
    meta_y[y] = meta_out[odd]
    got[LEFT, 0, 1] = block_to(OWN, LEFT, 1, right)
    got[RIGHT, 0, 0] = block_to(OWN, RIGHT, 0, left)
    for h in range(2):
        got[OWN, 1, h] = block_over(OWN, h)

    def add_spread(rel, c, h, first=False):
        term = nt_dot(xall[rel, c, h], space_v[rel, c, :, h * HALF : (h + 1) * HALF])
        if first:
            spread_v[...] = term
        else:
            spread_v[...] += term

    ld_space[OWN, 0].wait()
    add_spread(OWN, 0, 0, first=True)
    add_spread(OWN, 0, 1)
    for d in range(1, NX):
        from_y[d].wait_recv()
    line_out[0] = meta_y[0] + meta_y[1]
    line_out[1] = meta_y[2] + meta_y[3]
    from_z = [None] + [send(line_out, meta_z.at[z], tm=plus(d * NX)) for d in range(1, NX)]
    meta_z[z] = line_out[...]
    ld_space[OWN, 1].wait()
    for h in range(2):
        got[OWN, 1, h].wait_recv()
        add_spread(OWN, 1, h)
    ld_time.wait()
    time_t[...] = time_v[...].T.astype(BF16)
    for c in range(2):
        ld_space[OPP, c].wait()

        @pl.loop(0, COLS // BLK)
        def _(n, c=c):
            rows = pl.ds(pl.multiple_of(n * BLK, BLK), BLK)
            space_t[c, :, rows] = space_v[OPP, c, rows, :].T

    got[LEFT, 0, 0].wait_recv()
    got[OPP, 0, 0] = block_to(LEFT, OPP, 0, right)
    got[RIGHT, 0, 1].wait_recv()
    got[OPP, 0, 1] = block_to(RIGHT, OPP, 1, left)
    got[LEFT, 1, 0] = block_over(LEFT, 0)
    got[RIGHT, 1, 1] = block_over(RIGHT, 1)

    for rel, h in ((LEFT, 0), (RIGHT, 1)):
        ld_space[rel, 0].wait()
        add_spread(rel, 0, h)
    for rel, h in ((LEFT, 0), (RIGHT, 1)):
        ld_space[rel, 1].wait()
        got[rel, 1, h].wait_recv()
        add_spread(rel, 1, h)

    for d in range(1, NX):
        from_z[d].wait_recv()

    for d in range(NX):
        row = jnp.concatenate([meta_z[d, 0, 0:1, :], meta_z[d, 1, 0:1, :]], axis=1)
        when = lax.shift_right_arithmetic(row, 3)
        which = jnp.bitwise_and(row, 7)
        hot = lax.broadcasted_iota(jnp.int32, (TIMES, NX * SLOTS), 0) == when
        picked = nn_dot(time_t[...], jnp.where(hot, 1.0, 0.0).astype(BF16))
        slots = slice(d * NX * SLOTS, (d + 1) * NX * SLOTS)
        gt[:, slots] = picked.astype(BF16)
        picked_t = picked.T
        which_t = jnp.broadcast_to(which.astype(F32), (ROWS, NX * SLOTS)).T
        for b in range(NBLK):
            g4[slots, b * ROWS : (b + 1) * ROWS] = jnp.where(
                which_t == float(b), picked_t, 0.0
            ).astype(BF16)

    for rel, h in ((LEFT, 1), (RIGHT, 0)):
        got[rel, 0, h].wait_recv()
        got[rel, 1, h] = block_over(rel, h)
    for rel, h in ((LEFT, 1), (RIGHT, 0)):
        add_spread(rel, 0, h)
    for rel, h in ((LEFT, 1), (RIGHT, 0)):
        got[rel, 1, h].wait_recv()
        add_spread(rel, 1, h)
    for h in range(2):
        got[OPP, 0, h].wait_recv()
        got[OPP, 1, h] = block_over(OPP, h)
    for c in range(2):
        for h in range(2):
            if c:
                got[OPP, 1, h].wait_recv()
            spread = spread_v[...] + nn_dot(
                xall[OPP, c, h], space_t[c, h * HALF : (h + 1) * HALF, :]
            )
            if not (c and h):
                spread_v[...] = spread

    spread4 = jnp.concatenate(
        [spread[:, b * BLK : (b + 1) * BLK].astype(BF16) for b in range(NBLK)], axis=0
    )
    from_part = [None] * NTM
    for dz in (2, 1, 3, 0):
        there = lax.rem(z + NX - dz, NX)
        rows = pl.ds(pl.multiple_of(there * NX * SLOTS, NX * SLOTS), NX * SLOTS)
        part = nn_dot(g4[rows, :], spread4)
        part_out[pl.ds(there * NX, NX)] = part.astype(BF16).reshape(NX, SLOTS, BLK)
        for dy in (2, 1, 3, 0):
            e = dz * NX + dy
            if e:
                from_part[e] = send(part_out.at[minus(e)], part_in.at[e], tm=minus(e))

    for b in range(NBLK):
        for d in range(NX):
            which = jnp.bitwise_and(
                jnp.concatenate([meta_z[d, 0, 0:1, :], meta_z[d, 1, 0:1, :]], axis=1), 7
            )
            slots = slice(d * NX * SLOTS, (d + 1) * NX * SLOTS)
            gt4[b * ROWS : (b + 1) * ROWS, slots] = jnp.where(
                which == b, gt[:, slots].astype(F32), 0.0
            ).astype(BF16)
    ld_foot.wait()

    @pl.loop(0, SLOTS // 4)
    def _(k):
        for i in range(4):
            foot_t[4 * k + i] = foot_v[4 * k + i].T

    ld_obs.wait()
    pick = jnp.where(
        lax.broadcasted_iota(jnp.int32, (SLOTS, SLOTS), 0) == obs_v[...] - tm * SLOTS, 1.0, 0.0
    )
    pick_low = pick.astype(BF16)
    pick_t = pick.T.astype(BF16)
    ld_dep.wait()
    ld_weight.wait()

    flux = part_out[tm].astype(F32)
    for e in FAR_FIRST[::-1]:
        from_part[e].wait_recv()
        flux += part_in[e].astype(F32)
    flux = flux.astype(BF16)

    group = 16
    row16 = lax.broadcasted_iota(jnp.int32, (group, BLK), 0)
    for g in range(SLOTS // group):
        mine = flux[g * group : (g + 1) * group, :]
        acc = jnp.zeros((group, OBS), F32)
        for k in range(group):
            acc += nn_dot(jnp.where(row16 == k, mine, jnp.zeros_like(mine)), foot_t[g * group + k])
        sims_v[g * group : (g + 1) * group, :] = acc
    sims = sims_v[...]
    sims_hi = sims.astype(BF16)
    sims_lo = (sims - sims_hi.astype(F32)).astype(BF16)
    evolved = nn_dot(pick_low, sims_hi) + nn_dot(pick_low, sims_lo)
    evo_out[...] = evolved.astype(BF16)
    from_evo = []
    for rel, c in ((OPP, 1), (OPP, 0), (RIGHT, 1), (LEFT, 1), (RIGHT, 0), (LEFT, 0), (OWN, 1)):
        from_evo.append(send(evo_out, evo_in.at[len(from_evo)], space=at_x(rel, c)))
    for n in range(NSP - 1)[::-1]:
        from_evo[n].wait_recv()
        evolved += evo_in[n].astype(F32)
    depart = (weight_v[...] * (evolved - dep_v[...])).astype(BF16)
    mine_dep = nn_dot(pick_t, depart).astype(BF16)

    row16 = lax.broadcasted_iota(jnp.int32, (group, OBS), 0)
    for g in range(SLOTS // group):
        mine = mine_dep[g * group : (g + 1) * group, :]
        acc = jnp.zeros((group, BLK), F32)
        for k in range(group):
            acc += nn_dot(jnp.where(row16 == k, mine, jnp.zeros_like(mine)), foot_v[g * group + k])
        back_out[g * group : (g + 1) * group, :] = acc.astype(BF16)
    def back_copy(dest, source):
        return pltpu.make_async_remote_copy(
            src_ref=back_out,
            dst_ref=back_in.at[source],
            send_sem=bssem.at[dest],
            recv_sem=brsem.at[source],
            device_id={"tm": dest},
            device_id_type=MESH,
        )

    for d in range(NTM):

        @pl.when(tm != d)
        def _(d=d):
            back_copy(d, tm).start()

    back_in[tm] = back_out[...]
    left_here = len(sends)
    for copy in sends:
        copy.wait_send()

    adj = jnp.zeros((NBLK * ROWS, BLK), F32)
    for q in range(4):
        for e in range(4 * q, 4 * q + 4):

            @pl.when(tm != e)
            def _(e=e):
                back_copy(e, e).wait_recv()

        adj += nn_dot(
            gt4[:, q * 4 * SLOTS : (q + 1) * 4 * SLOTS],
            back_in[4 * q : 4 * q + 4].reshape(4 * SLOTS, BLK),
        )
    for b in range(NBLK):
        adj_v[:, b * BLK : (b + 1) * BLK] = adj[b * ROWS : (b + 1) * ROWS, :].astype(BF16)

    def terms(rel, c, h):
        return nn_dot(adj_v[...], space_v[rel, c, :, h * HALF : (h + 1) * HALF])

    from_pair = {}

    def to_sibling(rel, h):
        sib_out[rel, h] = terms(rel, 1, h).astype(BF16)
        from_pair[rel, h] = send(sib_out.at[rel, h], sib_in.at[rel, h], space=sibling)

    def own_terms(rel, h):
        term_v[rel, h] = terms(rel, 0, h)

    def pair(rel, h):
        from_pair[rel, h].wait_recv()
        return term_v[rel, h] + sib_in[rel, h].astype(F32)

    def hop(n, value, where):
        hop_out[n] = value.astype(BF16)
        return send(hop_out.at[n], hop_in.at[n], space=where)

    to_sibling(OPP, 0)
    to_sibling(OPP, 1)
    own_terms(OPP, 0)
    own_terms(OPP, 1)
    to_sibling(LEFT, 0)
    far_left = hop(0, pair(OPP, 0), right)
    far_right = hop(1, pair(OPP, 1), left)
    to_sibling(RIGHT, 1)
    own_terms(LEFT, 0)
    own_terms(RIGHT, 1)
    near_right = hop(2, pair(LEFT, 0), left)
    near_left = hop(3, pair(RIGHT, 1), right)
    to_sibling(RIGHT, 0)
    to_sibling(LEFT, 1)
    own_terms(RIGHT, 0)
    own_terms(LEFT, 1)
    term_v[RIGHT, 0] = pair(RIGHT, 0)
    term_v[LEFT, 1] = pair(LEFT, 1)
    to_sibling(OWN, 0)
    to_sibling(OWN, 1)
    for d in range(NTM):

        @pl.when(tm != d)
        def _(d=d):
            back_copy(d, tm).wait_send()

    far_left.wait_recv()
    last_left = hop(4, term_v[RIGHT, 0] + hop_in[0].astype(F32), right)
    far_right.wait_recv()
    last_right = hop(5, term_v[LEFT, 1] + hop_in[1].astype(F32), left)
    own_terms(OWN, 0)
    own_terms(OWN, 1)
    for h in range(2):
        cols = slice(h * HALF, (h + 1) * HALF)
        out_v[:, cols] = state_v[:, cols] + pair(OWN, h)
    for copy in sends[left_here:-2]:
        copy.wait_send()
    near_right.wait_recv()
    out_v[:, :HALF] += hop_in[2].astype(F32)
    near_left.wait_recv()
    out_v[:, HALF:] += hop_in[3].astype(F32)
    for h, copy in enumerate((last_left, last_right)):
        cols = slice(h * HALF, (h + 1) * HALF)
        copy.wait_recv()
        out_v[:, cols] += hop_in[4 + h].astype(F32)
    for copy in sends[-2:]:
        copy.wait_send()


N_LOADS = 17
N_SENDS = 3 + 3 + 6 + 8 + 15 + 7 + 8 + 6


def local(
    state,
    space_factor,
    time_factor,
    footprints,
    tile_obs,
    tile_block,
    tile_time,
    tile_count,
    obs_dep,
    obs_weight,
):
    any_spec = pl.BlockSpec(memory_space=pl.ANY)
    vm = pltpu.VMEM
    i32 = jnp.int32
    return pl.pallas_call(
        kernel,
        out_shape=pltpu.VMEM((ROWS, COLS), F32),
        in_specs=[any_spec] * 10,
        out_specs=pl.BlockSpec(memory_space=pltpu.VMEM),
        scratch_shapes=[
            vm((ROWS, COLS), F32),
            vm((NX, 2, COLS, COLS), BF16),
            vm((2, COLS, COLS), BF16),
            vm((TIMES, ROWS), F32),
            vm((SLOTS, OBS, BLK), BF16),
            vm((SLOTS, BLK, OBS), BF16),
            vm((1, SLOTS), i32),
            vm((1, SLOTS), i32),
            vm((1, SLOTS), i32),
            vm((1, 1), i32),
            vm((SLOTS, OBS), F32),
            vm((SLOTS, OBS), F32),
            vm((NX, 2, 2, ROWS, HALF), BF16),
            vm((ROWS, COLS), F32),
            vm((ROWS, TIMES), BF16),
            vm((2, 8, 2 * SLOTS), i32),
            vm((NX, 8, 2 * SLOTS), i32),
            vm((2, 8, 2 * SLOTS), i32),
            vm((NX, 2, 8, 2 * SLOTS), i32),
            vm((ROWS, NTM * SLOTS), BF16),
            vm((NBLK * ROWS, NTM * SLOTS), BF16),
            vm((NTM * SLOTS, NBLK * ROWS), BF16),
            vm((NTM, SLOTS, BLK), BF16),
            vm((NTM, SLOTS, BLK), BF16),
            vm((SLOTS, OBS), F32),
            vm((SLOTS, OBS), BF16),
            vm((NSP - 1, SLOTS, OBS), BF16),
            vm((SLOTS, BLK), BF16),
            vm((NTM, SLOTS, BLK), BF16),
            vm((ROWS, COLS), BF16),
            vm((NX, 2, ROWS, HALF), BF16),
            vm((NX, 2, ROWS, HALF), BF16),
            vm((NX, 2, ROWS, HALF), F32),
            vm((6, ROWS, HALF), BF16),
            vm((6, ROWS, HALF), BF16),
            pltpu.SemaphoreType.DMA((N_LOADS,)),
            pltpu.SemaphoreType.DMA((N_SENDS,)),
            pltpu.SemaphoreType.DMA((N_SENDS,)),
            pltpu.SemaphoreType.DMA((NTM,)),
            pltpu.SemaphoreType.DMA((NTM,)),
        ],
        compiler_params=pltpu.CompilerParams(
            collective_id=0, has_side_effects=True, vmem_limit_bytes=56 * 1024 * 1024
        ),
    )(
        state,
        space_factor,
        time_factor,
        footprints.reshape(SLOTS, OBS, BLK),
        tile_obs.reshape(1, SLOTS),
        tile_block.reshape(1, SLOTS),
        tile_time.reshape(1, SLOTS),
        tile_count,
        obs_dep,
        obs_weight,
    )


def solution(mesh):
    return jax.shard_map(
        local,
        mesh=mesh,
        in_specs=(
            P("tm", "space"),
            P("space", None),
            P(),
            P("tm", "space", None, None),
            P("tm", "space"),
            P("tm", "space"),
            P("tm", "space"),
            P("tm", "space"),
            P("tm", None),
            P("tm", None),
        ),
        out_specs=P("tm", "space"),
        check_vma=False,
    )
```
